256 devices in a mesh: lat: 8 (over y_hi, x), lon: 32 (over z, y_lo, core).
Axes of the slice: x: 4, y: 4 (y_hi: 2, y_lo: 2; y = y_hi * 2 + y_lo), z: 8, core: 2. Of those that a mesh axis runs over, the one named last changes fastest.
Arguments:
- atmosphere: float32 [32, 512, 4096], P(None, 'lat', 'lon'), may hold values from -6 to 6
- east_speed: float32 [512, 4096], P('lat', 'lon'), may hold values from -0.4 to 0.4
- north_speed: float32 [512, 4096], P('lat', 'lon'), may hold values from -0.4 to 0.4
- owners: int32 [2, 64, 1], replicated, may hold values from 0 to 31; in each aligned block of 64 rows (0 to 63, 64 to 127, ..., all dimensions but the last counted through in order) at most 4 rows name the same one
- cutoff: int32 [2, 64], replicated, may hold values from 128 to 2048, as said below
Outputs:
- advanced: float32 [32, 512, 4096], P(None, 'lat', 'lon')
- row_energy: float32 [8, 128], P('lat', 'lon')
The draws below stay inside these ranges and needn't reach their ends.
Inputs may be any that keep to these rules, and one draw needn't show every extreme that they name: `owners`: in each pole's 64 rows no longitude device is named more than 4 times; in some pole one is named exactly 4 times. Every pole has a row with cutoff exactly 2048.
All inputs are finite; a program needn't handle non-finite values.
Results may differ from the reference program's by a relative error of at most 0.0024.
Values may be sent and summed in bfloat16 or wider, within the bound.
No kernel may reach another device: no remote copies, remote signals or barrier semaphores. Data moves between devices by JAX's collectives and lax.ppermute only.
A program may use at most 64 MiB of HBM per device.

```python
import math
import jax
import jax.numpy as jnp
import numpy as np
from jax import lax

FIELDS = 4
LEV = 8
NLON = 4096
ROWS = 64
NLAT = 512
CAP = 4
N_LAT = 8
N_LON = 32


def draw_cutoff(key, part):
    key = jax.random.fold_in(key, 11)
    first_key, second_key = jax.random.split(key)
    values = jax.random.randint(first_key, (2, ROWS), NLON // 32, NLON // 2 + 1)
    chosen_spot = jax.random.randint(second_key, (2, 1), 0, ROWS)
    positions = jnp.arange(ROWS)[None, :]
    return jnp.where(positions == chosen_spot, NLON // 2, values).astype(jnp.int32)


def block_levels(rng, shape, cuts, smallest, top_value):
    gain = 1.0
    for axis_at, parts in cuts:
        steps = jax.random.uniform(jax.random.fold_in(jax.random.fold_in(rng, 6), axis_at), (parts,), jnp.float32, smallest / len(cuts), top_value / len(cuts))
        gain = gain * jnp.repeat(jnp.exp(steps), shape[axis_at] // parts).reshape((-1,) + (1,) * (len(shape) - 1 - axis_at))
    return gain


def shared_out(stream_key, own, number, rows, amount, top, bound, skew):
    sequence = jax.random.permutation(stream_key, amount)
    crowded, usual = load_shares(amount, rows * top, bound, skew, True), load_shares(amount, rows * top, bound, skew, False)
    places = jnp.arange(amount)

    def named(sizes, turn):
        used = int((sizes > 0).sum())
        fixed = max(1, used // 4)
        moved = fixed + (places - fixed + turn * (used - fixed)) % max(1, amount - fixed)
        return jnp.zeros((amount,), jnp.int32).at[sequence[jnp.where(places < fixed, places, moved)]].set(jnp.asarray(sizes, jnp.int32))

    sizes = jnp.where(number % 4 == 0, named(crowded, number // 4), named(usual, number - number // 4 - 1))
    mixed = jax.random.permutation(jax.random.fold_in(own, 3), amount)
    donor, sink = mixed[0:amount // 2 * 2:2], mixed[1:amount // 2 * 2:2]
    slack = jnp.minimum(sizes[donor] - 1, bound - sizes[sink]) // 2
    slack = jnp.where((donor == sequence[0]) | (sink == sequence[0]) | (sizes[sink] == 0), 0, jnp.maximum(slack, 0))
    moved = jax.random.randint(jax.random.fold_in(own, 4), (amount // 2,), 0, 1 << 20) % (slack + 1)
    sizes = sizes.at[donor].add(-moved).at[sink].add(moved)
    items = jnp.searchsorted(jnp.cumsum(sizes), jnp.arange(rows * top), side="right").astype(jnp.int32)
    grid = items.reshape(top, rows).T
    grid = grid[jax.random.permutation(jax.random.fold_in(own, 1), rows)]
    turn = jax.random.randint(jax.random.fold_in(own, 2), (rows, 1), 0, top)
    return jnp.take_along_axis(grid, (jnp.arange(top)[None, :] + turn) % top, axis=1)


def load_shares(count, total, limit, lean, full):
    loads = [(1 << 20) // math.isqrt(grade ** lean) + 1 for grade in range(1, count + 1)]
    largest = limit if full else min(limit, max(-(-total // count), total * loads[0] // sum(loads)))
    least = 1 if total - largest >= count - 1 else 0
    counts, spare = [largest] + [least] * (count - 1), total - largest - least * (count - 1)
    while spare > 0:
        movable = [i for i in range(1, count) if counts[i] < largest] or [i for i in range(1, count) if counts[i] < limit]
        whole, budget = sum([loads[i] for i in movable]), spare
        for i in movable:
            more = min(limit - counts[i], max(1, budget * loads[i] // whole), spare)
            counts[i] = counts[i] + more
            spare = spare - more
    return np.array(counts)


def noise(key, dims, spread, most, shards=(), held_as=jnp.bfloat16):
    loudness = block_levels(key, dims, shards, -0.22, 0.18) if shards else 1.0
    result = jax.random.normal(key, dims, jnp.float32) * spread * loudness
    return jnp.minimum(jnp.maximum(result, -most), most).astype(held_as)


def setup_inputs(seed: int = 0) -> dict:
    streams_of = jax.random.split(jax.random.key(seed), 6)
    atmosphere = noise(streams_of[0], (FIELDS * LEV, NLAT, NLON), 1.0, 6.0, ((1, 8), (2, 32)), jnp.float32)
    east_speed = jnp.clip(jax.random.uniform(streams_of[1], (NLAT, NLON), jnp.float32, -0.4, 0.4) * block_levels(streams_of[1], (NLAT, NLON), ((0, 8), (1, 32)), -0.4, 0.0), -0.4, 0.4)
    north_speed = jnp.clip(jax.random.uniform(streams_of[2], (NLAT, NLON), jnp.float32, -0.4, 0.4) * block_levels(streams_of[2], (NLAT, NLON), ((0, 8), (1, 32)), -0.4, 0.0), -0.4, 0.4)
    owners_keys = jax.random.split(jax.random.fold_in(streams_of[3], 1), 2 * ROWS // ROWS)
    owners_turns = jax.random.permutation(jax.random.fold_in(streams_of[3], 3), 2 * ROWS // ROWS)
    owners = jax.vmap(lambda own, number: shared_out(jax.random.fold_in(streams_of[3], 2), own, number, ROWS, N_LON, 1, CAP, 2))(owners_keys, owners_turns).reshape((2, ROWS, 1))
    cutoff = draw_cutoff(jax.random.fold_in(streams_of[5], 71), 0)
    return {"atmosphere": atmosphere, "east_speed": east_speed, "north_speed": north_speed, "owners": owners, "cutoff": cutoff}


diffusion_rate = 0.1


def transform_tables(first_freq, freq_count, length):
    frequency = first_freq + lax.iota(jnp.int32, freq_count)
    positions = lax.iota(jnp.int32, length)
    phase_steps = (positions[:, None] * frequency[None, :]) % length
    phases = phase_steps.astype(jnp.float32) * (2.0 * math.pi / length)
    return frequency, jnp.cos(phases).astype(jnp.bfloat16), jnp.sin(phases).astype(jnp.bfloat16)


def owner_slots(owner_row, capacity, lon_count):
    mine_hot = owner_row[:, None] == lax.iota(jnp.int32, lon_count)[None, :]
    owner_rank = jnp.sum(jnp.where(mine_hot, jnp.cumsum(mine_hot.astype(jnp.int32), axis=0) - 1, 0), axis=1)
    return owner_row * capacity + owner_rank


def reference(atmosphere, east_speed, north_speed, owners, cutoff):
    channels = FIELDS * LEV
    half_loop = NLON // 2
    pole_sign = jnp.where(lax.iota(jnp.int32, channels) < 2 * LEV, -1.0, 1.0).astype(jnp.float32)[:, None, None]
    top_row = jnp.roll(atmosphere[:, :1, :], half_loop, axis=2) * pole_sign
    bottom = jnp.roll(atmosphere[:, -1:, :], half_loop, axis=2) * pole_sign
    column = jnp.concatenate([top_row, atmosphere, bottom], axis=1)
    north_side = column[:, :-2]
    south_side = column[:, 2:]
    east_side = jnp.roll(atmosphere, -1, axis=2)
    west_side = jnp.roll(atmosphere, 1, axis=2)
    stepped = (atmosphere - 0.5 * east_speed * (east_side - west_side)
               - 0.5 * north_speed * (south_side - north_side)
               + diffusion_rate * (east_side + west_side + north_side + south_side - 4.0 * atmosphere))
    polar_rows = jnp.stack([stepped[:, :ROWS, :], stepped[:, NLAT - ROWS:, :]]).astype(jnp.bfloat16)
    flat_rows = polar_rows.reshape(2 * channels * ROWS, NLON).astype(jnp.float32)
    row_cut = jnp.broadcast_to(cutoff[:, None, :], (2, channels, ROWS)).reshape(-1)
    frequency, cos_table, sin_table = transform_tables(0, NLON // 2, NLON)
    cos_wide = cos_table.astype(jnp.float32)
    sin_wide = sin_table.astype(jnp.float32)
    highest = lax.Precision.HIGHEST
    coef_cos = jnp.dot(flat_rows, cos_wide, precision=highest)
    coef_sin = jnp.dot(flat_rows, sin_wide, precision=highest)
    weight = jnp.where(frequency == 0, 1.0 / NLON, 2.0 / NLON).astype(jnp.float32)
    kept_mask = frequency[None, :] < row_cut[:, None]
    kept_cos = jnp.where(kept_mask, coef_cos * weight, 0.0).astype(jnp.bfloat16).astype(jnp.float32)
    kept_sin = jnp.where(kept_mask, coef_sin * weight, 0.0).astype(jnp.bfloat16).astype(jnp.float32)
    filtered = jnp.dot(kept_cos, cos_wide.T, precision=highest) + jnp.dot(kept_sin, sin_wide.T, precision=highest)
    filtered = filtered.reshape(2, channels, ROWS, NLON)
    advanced = stepped.at[:, :ROWS, :].set(filtered[0]).at[:, NLAT - ROWS:, :].set(filtered[1])
    energy = jnp.mean(jnp.square(filtered), axis=(1, 3))
    energy_rows = []
    for pole_index in range(2):
        target_slot = owner_slots(owners[pole_index, :, 0], CAP, N_LON)
        chosen = (target_slot[None, :] == lax.iota(jnp.int32, N_LON * CAP)[:, None]).astype(jnp.float32)
        energy_rows.append(jnp.dot(chosen, energy[pole_index], precision=highest))
    row_energy = jnp.zeros((N_LAT, N_LON * CAP), jnp.float32)
    row_energy = row_energy.at[0].set(energy_rows[0]).at[N_LAT - 1].set(energy_rows[1])
    return advanced, row_energy
```

```python
import functools
import math

import jax
import jax.numpy as jnp
import ml_dtypes
import numpy as np
from jax import lax
from jax.experimental import pallas as pl
from jax.experimental.pallas import tpu as pltpu
from jax.sharding import PartitionSpec as P

LEV = 8
DIFFUSION = 0.1
CAP = 4
VMEM = pl.BlockSpec(memory_space=pltpu.VMEM)


def real_forward(values):
    n = len(values)
    if n == 1:
        return [(values[0], None)]
    even = real_forward(values[0::2])
    odd = real_forward(values[1::2])
    half = n // 2
    out = [None] * (half + 1)
    for k in range(half // 2 + 1):
        er, ei = even[k]
        orr, oi = odd[k]
        if k == 0:
            out[0] = (er + orr, None)
            out[half] = (er - orr, None)
        elif 2 * k == half:
            out[k] = (er, -orr)
        else:
            c, s = math.cos(2 * math.pi * k / n), math.sin(2 * math.pi * k / n)
            if 8 * k == n:
                tr, ti = (orr + oi) * c, (oi - orr) * c
            else:
                tr, ti = orr * c + oi * s, oi * c - orr * s
            out[k] = (er + tr, ei + ti)
            out[half - k] = (er - tr, ti - ei)
    return out


def real_inverse(coefs):
    half = len(coefs) - 1
    if half == 0:
        return [coefs[0][0]]
    n = 2 * half
    even, odd = [None] * (half // 2 + 1), [None] * (half // 2 + 1)
    for k in range(half // 2 + 1):
        ar, ai = coefs[k]
        br, bi = coefs[half - k]
        if k == 0:
            even[0], odd[0] = (ar + br, None), (ar - br, None)
        elif 2 * k == half:
            even[k], odd[k] = (ar + ar, None), (-(ai + ai), None)
        else:
            even[k] = (ar + br, ai - bi)
            dr, di = ar - br, ai + bi
            c, s = math.cos(2 * math.pi * k / n), math.sin(2 * math.pi * k / n)
            if 8 * k == n:
                odd[k] = ((dr - di) * c, (dr + di) * c)
            else:
                odd[k] = (dr * c - di * s, di * c + dr * s)
    if half == 1:
        return [even[0][0], odd[0][0]]
    first, second = real_inverse(even), real_inverse(odd)
    return [v for pair in zip(first, second) for v in pair]


@functools.lru_cache(None)
def tables(parts, width):
    length = parts * width
    steps = np.arange(width)[:, None] * np.arange(width)[None, :] % width
    angle = 2 * np.pi * steps / width
    cos, sin = np.cos(angle), np.sin(angle)
    forward = np.block([[cos, -sin], [sin, cos]])
    inverse = forward.T / length

    def halves(table):
        high = table.astype(ml_dtypes.bfloat16)
        low = (table - high.astype(np.float64)).astype(ml_dtypes.bfloat16)
        return np.stack([high, low])

    turn = 2 * np.pi * np.arange(parts // 2 + 1)[:, None] * np.arange(width)[None, :] / length
    twiddle = np.stack([np.cos(turn), np.sin(turn)]).astype(np.float32)
    return np.stack([halves(forward), halves(inverse)]), twiddle


def split_halves(value):
    high = value.astype(jnp.bfloat16)
    return high, (value - high.astype(jnp.float32)).astype(jnp.bfloat16)


def filter_kernel(
    parts, rows_ref, cut_ref, slot_ref, mat_ref, tw_ref, out_ref, energy_ref, high_ref, low_ref, wave_ref
):
    count = parts // 2 + 1
    row_count, width = rows_ref.shape[1], rows_ref.shape[2]

    def first(block, carry):
        at = pl.ds(pl.multiple_of(block * 16, 16), 16)
        halves = []
        for part in range(2):
            values = [
                rows_ref[s, at, :].astype(jnp.float32)[part * 8 : part * 8 + 8] for s in range(parts)
            ]
            turned = []
            for k, (re, im) in enumerate(real_forward(values)):
                if k == 0:
                    turned.append((re, jnp.zeros_like(re)))
                    continue
                c, s = tw_ref[0, k : k + 1, :], tw_ref[1, k : k + 1, :]
                if im is None:
                    turned.append((re * c, -(re * s)))
                else:
                    turned.append((re * c + im * s, im * c - re * s))
            halves.append(turned)
        for k in range(count):
            for side in range(2):
                value = jnp.concatenate([halves[0][k][side], halves[1][k][side]], axis=0)
                high, low = split_halves(value)
                lanes = slice(side * width, (side + 1) * width)
                high_ref[k, at, lanes] = high
                low_ref[k, at, lanes] = low
        return carry

    lax.fori_loop(0, row_count // 16, first, 0)

    cut = cut_ref[...]
    lane = lax.broadcasted_iota(jnp.int32, (row_count, width), 1)
    for k in range(count):
        high, low = high_ref[k], low_ref[k]
        dot = functools.partial(jnp.dot, preferred_element_type=jnp.float32)
        coef = dot(high, mat_ref[0, 0]) + dot(low, mat_ref[0, 0]) + dot(high, mat_ref[0, 1])
        wave = k + parts * lane
        keep = jnp.minimum(wave, parts * width - wave) < cut
        keep = jnp.concatenate([keep, keep], axis=1)
        high, low = split_halves(jnp.where(keep, coef, 0.0))
        wave_ref[k] = dot(high, mat_ref[1, 0]) + dot(low, mat_ref[1, 0]) + dot(high, mat_ref[1, 1])

    slot_lane = lax.broadcasted_iota(jnp.int32, (8, width), 1)

    def last(block, energy):
        at = pl.ds(pl.multiple_of(block * 16, 16), 16)
        halves = []
        for part in range(2):
            here = pl.ds(pl.multiple_of(block * 16 + part * 8, 8), 8)
            coefs = []
            for k in range(count):
                re, im = wave_ref[k, here, :width], wave_ref[k, here, width:]
                if k == 0:
                    coefs.append((re, None))
                    continue
                c, s = tw_ref[0, k : k + 1, :], tw_ref[1, k : k + 1, :]
                coefs.append((re * c - im * s, None if 2 * k == parts else im * c + re * s))
            values = real_inverse(coefs)
            total = values[0] * values[0]
            for value in values[1:]:
                total = total + value * value
            row_sum = jnp.sum(total, axis=1, keepdims=True)
            energy = energy + jnp.where(slot_ref[here, :] == slot_lane, row_sum, 0.0)
            halves.append(values)
        for s in range(parts):
            out_ref[s, at, :] = jnp.concatenate([halves[0][s], halves[1][s]], axis=0).astype(jnp.bfloat16)
        return energy

    energy_ref[...] = lax.fori_loop(0, row_count // 16, last, jnp.zeros((8, width), jnp.float32))


def filter_rows(rows, cut, slot):
    parts, row_count, width = rows.shape
    count = parts // 2 + 1
    mats, twiddle = tables(parts, width)
    return pl.pallas_call(
        functools.partial(filter_kernel, parts),
        out_shape=(
            jax.ShapeDtypeStruct(rows.shape, jnp.bfloat16),
            jax.ShapeDtypeStruct((8, width), jnp.float32),
        ),
        in_specs=[VMEM] * 5,
        out_specs=(VMEM, VMEM),
        scratch_shapes=[
            pltpu.VMEM((count, row_count, 2 * width), jnp.bfloat16),
            pltpu.VMEM((count, row_count, 2 * width), jnp.bfloat16),
            pltpu.VMEM((count, row_count, 2 * width), jnp.float32),
        ],
        compiler_params=pltpu.CompilerParams(vmem_limit_bytes=32 * 1024 * 1024),
    )(rows, cut, slot, jnp.asarray(mats), jnp.asarray(twiddle))


def edges_kernel(field_ref, first_ref, last_ref):
    channels, row_count, width = field_ref.shape
    lane = lax.broadcasted_iota(jnp.int32, (row_count, width), 1)
    first = jnp.zeros((row_count, width), jnp.float32)
    last = jnp.zeros((row_count, width), jnp.float32)
    for c in range(channels):
        cells = field_ref[c]
        here = lane == c
        first = jnp.where(here, cells if c == 0 else pltpu.roll(cells, c, 1), first)
        last = jnp.where(here, pltpu.roll(cells, c + 1, 1), last)
    first_ref[...] = first[:, :channels]
    last_ref[...] = last[:, :channels]


def edge_columns(field):
    channels, row_count, _ = field.shape
    shape = jax.ShapeDtypeStruct((row_count, channels), jnp.float32)
    return pl.pallas_call(
        edges_kernel, out_shape=(shape, shape), in_specs=[VMEM], out_specs=(VMEM, VMEM)
    )(field)


def step_kernel(field_ref, east_ref, north_ref, up_ref, down_ref, west_col_ref, east_col_ref, full_ref, short_ref):
    channels, row_count, width = field_ref.shape
    lane = lax.broadcasted_iota(jnp.int32, (row_count, width), 1)
    row = lax.broadcasted_iota(jnp.int32, (row_count, width), 0)
    east, north = 0.5 * east_ref[...], 0.5 * north_ref[...]
    to_east, to_west = DIFFUSION - east, DIFFUSION + east
    to_south, to_north = DIFFUSION - north, DIFFUSION + north
    pad = jnp.zeros((row_count, width - channels), jnp.float32)
    west_col = jnp.concatenate([west_col_ref[...], pad], axis=1)
    east_col = jnp.concatenate([east_col_ref[...], pad], axis=1)
    for c in range(channels):
        cells = field_ref[c]
        west = jnp.where(lane == 0, pltpu.roll(west_col, (width - c) % width, 1), pltpu.roll(cells, 1, 1))
        east = jnp.where(
            lane == width - 1, pltpu.roll(east_col, width - 1 - c, 1), pltpu.roll(cells, width - 1, 1)
        )
        up = jnp.where(row == 0, up_ref[c : c + 1, :], pltpu.roll(cells, 1, 0))
        down = jnp.where(row == row_count - 1, down_ref[c : c + 1, :], pltpu.roll(cells, row_count - 1, 0))
        stepped = (
            (1.0 - 4.0 * DIFFUSION) * cells + to_east * east + to_west * west + to_south * down + to_north * up
        )
        full_ref[c] = stepped
        short_ref[c] = stepped.astype(jnp.bfloat16)


def step(field, east_speed, north_speed, up, down, west_col, east_col):
    return pl.pallas_call(
        step_kernel,
        out_shape=(
            jax.ShapeDtypeStruct(field.shape, jnp.float32),
            jax.ShapeDtypeStruct(field.shape, jnp.bfloat16),
        ),
        in_specs=[VMEM] * 7,
        out_specs=(VMEM, VMEM),
        compiler_params=pltpu.CompilerParams(vmem_limit_bytes=32 * 1024 * 1024),
    )(field, east_speed, north_speed, up, down, west_col, east_col)


def on_device(lat_count, lon_count, atmosphere, east_speed, north_speed, owners, cutoff):
    channels, row_count, width = atmosphere.shape
    band = lax.axis_index("lat")
    mine = lax.axis_index("lon")
    top, bottom = band == 0, band == lat_count - 1
    is_polar = jnp.logical_or(top, bottom)
    even = band % 2 == 0

    first_row, last_row = atmosphere[:, 0], atmosphere[:, -1]
    sign = jnp.where(lax.iota(jnp.int32, channels) < 2 * LEV, -1.0, 1.0).astype(jnp.float32)[:, None]
    outward = jnp.where(even, first_row, last_row)
    outward = jnp.where(is_polar, outward * sign, outward)
    inward = jnp.where(even, last_row, first_row)
    pairs_out, pairs_in = [], []
    for b in range(lat_count):
        for o in range(lon_count):
            here = b * lon_count + o
            if b == 0 or b == lat_count - 1:
                pairs_out.append((here, b * lon_count + (o + lon_count // 2) % lon_count))
            else:
                pairs_out.append((here, (b + 1 if b % 2 else b - 1) * lon_count + o))
            pairs_in.append((here, (b - 1 if b % 2 else b + 1) * lon_count + o))
    got_out = lax.ppermute(outward, ("lat", "lon"), pairs_out)
    got_in = lax.ppermute(inward, ("lat", "lon"), pairs_in)
    up = jnp.where(even, got_out, got_in)
    down = jnp.where(even, got_in, got_out)

    first_col, last_col = edge_columns(atmosphere)
    west_col = lax.ppermute(last_col, "lon", [(o, (o + 1) % lon_count) for o in range(lon_count)])
    east_col = lax.ppermute(first_col, "lon", [((o + 1) % lon_count, o) for o in range(lon_count)])
    full, short = step(atmosphere, east_speed, north_speed, up, down, west_col, east_col)

    owner_row = jnp.where(bottom, owners[1, :, 0], owners[0, :, 0])
    cut_row = jnp.where(bottom, cutoff[1], cutoff[0])
    same = owner_row[:, None] == owner_row[None, :]
    earlier = lax.iota(jnp.int32, row_count)[:, None] > lax.iota(jnp.int32, row_count)[None, :]
    rank = jnp.sum(jnp.logical_and(same, earlier).astype(jnp.int32), axis=1)
    slot = owner_row * CAP + rank

    received = lax.all_to_all(short, "lon", split_axis=0, concat_axis=0, tiled=True)
    filtered, energy = filter_rows(received, cut_row[:, None], slot[:, None])
    returned = lax.all_to_all(filtered, "lon", split_axis=0, concat_axis=0, tiled=True)
    energy = jnp.sum(energy, axis=0) * (1.0 / (channels * lon_count * width))
    energy = lax.psum(energy, "lon")
    advanced = jnp.where(is_polar, returned.astype(jnp.float32), full)
    row_energy = lax.dynamic_slice_in_dim(energy, mine * CAP, CAP)
    row_energy = jnp.where(is_polar, row_energy, 0.0)[None, :]
    return advanced, row_energy


def solution(mesh):
    in_specs = (P(None, "lat", "lon"), P("lat", "lon"), P("lat", "lon"), P(), P())
    out_specs = (P(None, "lat", "lon"), P("lat", "lon"))
    return jax.shard_map(
        functools.partial(on_device, mesh.shape["lat"], mesh.shape["lon"]),
        mesh=mesh,
        in_specs=in_specs,
        out_specs=out_specs,
        check_vma=False,
    )
```

```python
import functools
import math

import jax
import jax.numpy as jnp
import ml_dtypes
import numpy as np
from jax import lax
from jax.experimental import pallas as pl
from jax.experimental.pallas import tpu as pltpu
from jax.sharding import PartitionSpec as P

LEV = 8
DIFFUSION = 0.1
CAP = 4
EXTRA = 8
VMEM = pl.BlockSpec(memory_space=pltpu.VMEM)


def real_forward(values):
    n = len(values)
    if n == 1:
        return [(values[0], None)]
    even = real_forward(values[0::2])
    odd = real_forward(values[1::2])
    half = n // 2
    out = [None] * (half + 1)
    for k in range(half // 2 + 1):
        er, ei = even[k]
        orr, oi = odd[k]
        if k == 0:
            out[0] = (er + orr, None)
            out[half] = (er - orr, None)
        elif 2 * k == half:
            out[k] = (er, -orr)
        else:
            c, s = math.cos(2 * math.pi * k / n), math.sin(2 * math.pi * k / n)
            if 8 * k == n:
                tr, ti = (orr + oi) * c, (oi - orr) * c
            else:
                tr, ti = orr * c + oi * s, oi * c - orr * s
            out[k] = (er + tr, ei + ti)
            out[half - k] = (er - tr, ti - ei)
    return out


def real_inverse(coefs):
    half = len(coefs) - 1
    if half == 0:
        return [coefs[0][0]]
    n = 2 * half
    even, odd = [None] * (half // 2 + 1), [None] * (half // 2 + 1)
    for k in range(half // 2 + 1):
        ar, ai = coefs[k]
        br, bi = coefs[half - k]
        if k == 0:
            even[0], odd[0] = (ar + br, None), (ar - br, None)
        elif 2 * k == half:
            even[k], odd[k] = (ar + ar, None), (-(ai + ai), None)
        else:
            even[k] = (ar + br, ai - bi)
            dr, di = ar - br, ai + bi
            c, s = math.cos(2 * math.pi * k / n), math.sin(2 * math.pi * k / n)
            if 8 * k == n:
                odd[k] = ((dr - di) * c, (dr + di) * c)
            else:
                odd[k] = (dr * c - di * s, di * c + dr * s)
    if half == 1:
        return [even[0][0], odd[0][0]]
    first, second = real_inverse(even), real_inverse(odd)
    return [v for pair in zip(first, second) for v in pair]


@functools.lru_cache(None)
def tables(parts, width):
    length = parts * width
    steps = np.arange(width)[:, None] * np.arange(width)[None, :] % width
    angle = 2 * np.pi * steps / width
    cos, sin = np.cos(angle), np.sin(angle)
    forward = np.block([[cos, -sin], [sin, cos]])
    inverse = forward.T / length

    def halves(table):
        high = table.astype(ml_dtypes.bfloat16)
        low = (table - high.astype(np.float64)).astype(ml_dtypes.bfloat16)
        return np.stack([high, low])

    turn = 2 * np.pi * np.arange(parts // 2 + 1)[:, None] * np.arange(width)[None, :] / length
    twiddle = np.stack([np.cos(turn), np.sin(turn)]).astype(np.float32)
    return np.stack([halves(forward), halves(inverse)]), twiddle


def split_halves(value):
    high = value.astype(jnp.bfloat16)
    return high, (value - high.astype(jnp.float32)).astype(jnp.bfloat16)


def add_edges(values, edge, lane):
    width = lane.shape[1]
    rim = jnp.logical_or(lane == 0, lane == width - 1)
    return [
        value + jnp.where(rim, pltpu.roll(edge, (width - 2 * s - 1) % width, 1), 0.0)
        for s, value in enumerate(values)
    ]


def filter_kernel(
    parts, first_block, block_count, flags_ref, rows_ref, halo_ref, cut_ref, slot_ref, mat_ref, tw_ref, *refs
):
    last_call = first_block + block_count == 4
    if last_call:
        done_ref, before_ref, out_ref, extra_ref, pair_ref, edge_ref, high_ref, low_ref, wave_ref = refs
    else:
        out_ref, energy_ref, extra_ref, pair_ref, edge_ref, high_ref, low_ref, wave_ref = refs
    count = parts // 2 + 1
    row_count, width = rows_ref.shape[1] - EXTRA, rows_ref.shape[2]
    bottom = flags_ref[0] == 1
    rows_here = 16 * block_count

    for s in range(parts):
        extra_ref[s * EXTRA : (s + 1) * EXTRA, :] = rows_ref[s, row_count : row_count + EXTRA, :].astype(jnp.float32)

    def extra(i):
        return extra_ref[pl.ds(i, parts, stride=EXTRA), :]

    turned = pltpu.roll(extra(0), width // 2, 1)
    coef = extra(1)
    from_west = coef * pltpu.roll(turned, 1, 0)
    from_east = pltpu.roll(coef * pltpu.roll(turned, parts - 1, 0), width // 2, 1)
    pair_ref[pl.ds(0, parts, stride=2), :] = from_east
    pair_ref[pl.ds(1, parts, stride=2), :] = from_west
    edge = pair_ref[...].T[:row_count, :]
    edge_ref[...] = jnp.concatenate([edge, jnp.zeros((row_count, width - 2 * parts), jnp.float32)], axis=1)
    if last_call:
        border = extra(5) * halo_ref[...].astype(jnp.float32)
        border_row = jnp.where(bottom, 0, 15)
    else:
        border = extra(3) * pltpu.roll(extra(2), parts // 2, 0)
        border_row = jnp.where(bottom, 15, 0)
    lane = lax.broadcasted_iota(jnp.int32, (8, width), 1)
    sub = lax.broadcasted_iota(jnp.int32, (8, width), 0)

    for block in range(block_count):
        at = slice(16 * block, 16 * block + 16)
        source = first_block + block
        natural = jnp.where(bottom, 48 - 16 * source, 16 * source)
        has_border = source == (3 if last_call else 0)
        halves = []
        for part in range(2):
            values = [
                rows_ref[s, 16 * source : 16 * source + 16, :].astype(jnp.float32)[part * 8 : part * 8 + 8]
                for s in range(parts)
            ]
            values = add_edges(values, edge_ref[pl.ds(pl.multiple_of(natural + 8 * part, 8), 8), :], lane)
            if has_border:
                here = sub + 8 * part == border_row
                values = [v + jnp.where(here, border[s : s + 1, :], 0.0) for s, v in enumerate(values)]
            spun = []
            for k, (re, im) in enumerate(real_forward(values)):
                if k == 0:
                    spun.append((re, jnp.zeros_like(re)))
                    continue
                c, sn = tw_ref[0, k : k + 1, :], tw_ref[1, k : k + 1, :]
                if im is None:
                    spun.append((re * c, -(re * sn)))
                else:
                    spun.append((re * c + im * sn, im * c - re * sn))
            halves.append(spun)
        for k in range(count):
            for side in range(2):
                value = jnp.concatenate([halves[0][k][side], halves[1][k][side]], axis=0)
                high, low = split_halves(value)
                lanes = slice(side * width, (side + 1) * width)
                high_ref[k, at, lanes] = high
                low_ref[k, at, lanes] = low

    cut = cut_ref[16 * first_block : 16 * first_block + rows_here, :]
    wide = lax.broadcasted_iota(jnp.int32, (rows_here, 2 * width), 1) % width
    dot = functools.partial(jnp.dot, preferred_element_type=jnp.float32)
    step = 6 if block_count > 1 else count
    for k0 in range(0, count, step):
        k1 = min(count, k0 + step)
        flat = ((k1 - k0) * rows_here, 2 * width)
        high, low = high_ref[k0:k1].reshape(flat), low_ref[k0:k1].reshape(flat)
        coef = dot(high, mat_ref[0, 0]) + dot(low, mat_ref[0, 0]) + dot(high, mat_ref[0, 1])
        kept = []
        for k in range(k0, k1):
            wave = k + parts * wide
            keep = jnp.minimum(wave, parts * width - wave) < cut
            kept.append(jnp.where(keep, coef[(k - k0) * rows_here : (k - k0 + 1) * rows_here], 0.0))
        high, low = split_halves(jnp.concatenate(kept, axis=0))
        wave = dot(high, mat_ref[1, 0]) + dot(low, mat_ref[1, 0]) + dot(high, mat_ref[1, 1])
        wave_ref[k0:k1] = wave.reshape(k1 - k0, rows_here, 2 * width)

    if last_call:
        for s in range(parts):
            out_ref[s, : 16 * first_block, :] = done_ref[s]
    energy = before_ref[...] if last_call else jnp.zeros((8, width), jnp.float32)
    for block in range(block_count):
        source = first_block + block
        halves = []
        for part in range(2):
            here = slice(16 * block + 8 * part, 16 * block + 8 * part + 8)
            coefs = []
            for k in range(count):
                re, im = wave_ref[k, here, :width], wave_ref[k, here, width:]
                if k == 0:
                    coefs.append((re, None))
                    continue
                c, sn = tw_ref[0, k : k + 1, :], tw_ref[1, k : k + 1, :]
                coefs.append((re * c - im * sn, None if 2 * k == parts else im * c + re * sn))
            values = real_inverse(coefs)
            total = values[0] * values[0]
            for value in values[1:]:
                total = total + value * value
            row_sum = jnp.sum(total, axis=1, keepdims=True)
            slots = slot_ref[16 * source + 8 * part : 16 * source + 8 * part + 8, :]
            energy = energy + jnp.where(slots == lane, row_sum, 0.0)
            halves.append(values)
        for s in range(parts):
            out_ref[s, 16 * source : 16 * source + 16, :] = jnp.concatenate(
                [halves[0][s], halves[1][s]], axis=0
            ).astype(jnp.bfloat16)
    if last_call:
        total = jnp.sum(energy, axis=0, keepdims=True)
        high = total.astype(jnp.bfloat16).astype(jnp.float32)
        tail = jnp.where(sub == 0, high, jnp.where(sub == 1, total - high, 0.0)).astype(jnp.bfloat16)
        for s in range(parts):
            out_ref[s, row_count : row_count + EXTRA, :] = tail
    else:
        energy_ref[...] = energy


def filter_rows(flags, rows, halo, cut, slot):
    parts, row_count, width = rows.shape
    row_count -= EXTRA
    count = parts // 2 + 1
    mats, twiddle = tables(parts, width)
    operands = (cut, slot, jnp.asarray(mats), jnp.asarray(twiddle))

    def call(first_block, block_count, out_shape, *args):
        rows_here = 16 * block_count
        return pl.pallas_call(
            functools.partial(filter_kernel, parts, first_block, block_count),
            out_shape=out_shape,
            in_specs=[pl.BlockSpec(memory_space=pltpu.SMEM)] + [VMEM] * (len(args) - 1),
            out_specs=jax.tree.map(lambda _: VMEM, out_shape),
            scratch_shapes=[
                pltpu.VMEM((parts * EXTRA, width), jnp.float32),
                pltpu.VMEM((2 * parts, width), jnp.float32),
                pltpu.VMEM((row_count, width), jnp.float32),
                pltpu.VMEM((count, rows_here, 2 * width), jnp.bfloat16),
                pltpu.VMEM((count, rows_here, 2 * width), jnp.bfloat16),
                pltpu.VMEM((count, rows_here, 2 * width), jnp.float32),
            ],
            compiler_params=pltpu.CompilerParams(vmem_limit_bytes=24 * 1024 * 1024),
            cost_estimate=pl.CostEstimate(
                flops=rows_here * parts * width * 8000, bytes_accessed=rows.size * 4, transcendentals=0
            ),
        )(*args)

    done = jax.ShapeDtypeStruct((parts, row_count - 16, width), jnp.bfloat16)
    whole = jax.ShapeDtypeStruct(rows.shape, jnp.bfloat16)
    energy = jax.ShapeDtypeStruct((8, width), jnp.float32)
    halo_rows = halo(rows)
    out, part = call(0, 3, (done, energy), flags, rows, jnp.zeros((8, width), jnp.bfloat16), *operands)
    return call(3, 1, whole, flags, rows, halo_rows, *operands, out, part)


def partial_kernel(flags_ref, field_ref, east_ref, north_ref, out_ref, acc_ref):
    channels, row_count, width = field_ref.shape
    lane = lax.broadcasted_iota(jnp.int32, (row_count, width), 1)
    row = lax.broadcasted_iota(jnp.int32, (row_count, width), 0)
    bottom = flags_ref[0] == 1
    lower = flags_ref[1] == 1
    east, north = 0.5 * east_ref[...], 0.5 * north_ref[...]
    to_east, to_west = DIFFUSION - east, DIFFUSION + east
    to_south, to_north = DIFFUSION - north, DIFFUSION + north
    mid_east = jnp.where(lane == width - 1, 0.0, to_east)
    mid_west = jnp.where(lane == 0, 0.0, to_west)
    mid_south = jnp.where(row == row_count - 1, 0.0, to_south)
    mid_north = jnp.where(row == 0, 0.0, to_north)
    acc = jnp.zeros((row_count, width), jnp.float32)
    for c in range(channels):
        cells = field_ref[c]
        here = jnp.logical_or(lane == 2 * c, lane == 2 * c + 1)
        acc = jnp.where(here, pltpu.roll(cells, 2 * c + 1, 1), acc)
        stepped = (
            (1.0 - 4.0 * DIFFUSION) * cells
            + mid_east * pltpu.roll(cells, width - 1, 1)
            + mid_west * pltpu.roll(cells, 1, 1)
            + mid_south * pltpu.roll(cells, row_count - 1, 0)
            + mid_north * pltpu.roll(cells, 1, 0)
        ).astype(jnp.bfloat16)
        for t in range(row_count // 16):
            at = jnp.where(bottom, row_count - 16 - 16 * t, 16 * t)
            out_ref[c, pl.ds(pl.multiple_of(at, 16), 16), :] = stepped[16 * t : 16 * t + 16]
    coef = jnp.where(lane == 0, to_west, to_east)
    rim = jnp.where(lane == 2 * channels + 1, pltpu.roll(to_west, 2 * channels + 1, 1), 0.0)
    rim = jnp.where(lane == 2 * channels, pltpu.roll(to_east, 2 * channels + 1, 1), rim)
    acc_ref[...] = jnp.where(lane < 2 * channels, acc, rim).T
    last = acc_ref[pl.ds(0, channels, stride=2), :]
    first = acc_ref[pl.ds(1, channels, stride=2), :]
    edges = jnp.concatenate([first, last], axis=1)
    rim_first = acc_ref[2 * channels + 1 : 2 * channels + 2, :]
    rim_last = acc_ref[2 * channels : 2 * channels + 1, :]
    rim = jnp.concatenate([rim_first, rim_last], axis=1)
    outer = jnp.where(bottom, to_south[row_count - 1 :, :], to_north[:1, :])
    inner = jnp.where(bottom, to_north[:1, :], to_south[row_count - 1 :, :])
    sub = lax.broadcasted_iota(jnp.int32, (EXTRA, width), 0)
    for c in range(channels):
        top_row, low_row = field_ref[c, 0:1, :], field_ref[c, row_count - 1 : row_count, :]
        tail = jnp.where(sub == 0, edges[c : c + 1, :], 0.0)
        tail = jnp.where(sub == 1, rim, tail)
        tail = jnp.where(sub == 2, jnp.where(bottom, low_row, top_row), tail)
        tail = jnp.where(sub == 3, -outer if c < 2 * LEV else outer, tail)
        tail = jnp.where(sub == 4, jnp.where(lower, low_row, top_row), tail)
        tail = jnp.where(sub == 5, inner, tail)
        out_ref[c, row_count : row_count + EXTRA, :] = tail.astype(jnp.bfloat16)


def partial_step(flags, field, east_speed, north_speed):
    channels, row_count, width = field.shape
    return pl.pallas_call(
        partial_kernel,
        out_shape=jax.ShapeDtypeStruct((channels, row_count + EXTRA, width), jnp.bfloat16),
        in_specs=[pl.BlockSpec(memory_space=pltpu.SMEM)] + [VMEM] * 3,
        out_specs=VMEM,
        scratch_shapes=[pltpu.VMEM((width, row_count), jnp.float32)],
        compiler_params=pltpu.CompilerParams(vmem_limit_bytes=16 * 1024 * 1024),
        cost_estimate=pl.CostEstimate(flops=field.size * 9, bytes_accessed=field.size * 6, transcendentals=0),
    )(flags, field, east_speed, north_speed)


def merge_kernel(flags_ref, back_ref, full_ref, out_ref, energy_ref, wide_ref, sems):
    del full_ref
    channels, row_count, width = out_ref.shape
    bottom = flags_ref[0] == 1
    polar = flags_ref[2] == 1
    group = 8

    @pl.when(polar)
    def _():
        copies = []
        for g in range(channels // group):
            for c in range(g * group, (g + 1) * group):
                for t in range(row_count // 16):
                    at = jnp.where(bottom, row_count - 16 - 16 * t, 16 * t)
                    wide_ref[c, 16 * t : 16 * t + 16, :] = back_ref[
                        c, pl.ds(pl.multiple_of(at, 16), 16), :
                    ].astype(jnp.float32)
            here = pl.ds(g * group, group)
            copies.append(pltpu.make_async_copy(wide_ref.at[here], out_ref.at[here], sems.at[g]))
            copies[-1].start()
        total = jnp.zeros((EXTRA, width), jnp.float32)
        for c in range(channels):
            total = total + back_ref[c, row_count : row_count + EXTRA, :].astype(jnp.float32)
        energy = jnp.sum(total, axis=0, keepdims=True) * (1.0 / (channels * channels * width))
        energy = pltpu.roll(jnp.broadcast_to(energy, (8, width)), flags_ref[3], 1)
        energy_ref[...] = energy[:1, :CAP]
        for copy in copies:
            copy.wait()

    @pl.when(jnp.logical_not(polar))
    def _():
        energy_ref[...] = jnp.zeros((1, CAP), jnp.float32)


def merge(flags, back, full):
    channels, row_count, width = full.shape
    anywhere = pl.BlockSpec(memory_space=pl.ANY)
    return pl.pallas_call(
        merge_kernel,
        out_shape=(
            jax.ShapeDtypeStruct(full.shape, jnp.float32),
            jax.ShapeDtypeStruct((1, CAP), jnp.float32),
        ),
        in_specs=[pl.BlockSpec(memory_space=pltpu.SMEM), VMEM, anywhere],
        out_specs=(anywhere, VMEM),
        input_output_aliases={2: 0},
        scratch_shapes=[pltpu.VMEM(full.shape, jnp.float32), pltpu.SemaphoreType.DMA((channels // 8,))],
        compiler_params=pltpu.CompilerParams(vmem_limit_bytes=16 * 1024 * 1024),
    )(flags, back, full)


def edges_kernel(field_ref, first_ref, last_ref):
    channels, row_count, width = field_ref.shape
    lane = lax.broadcasted_iota(jnp.int32, (row_count, width), 1)
    first = jnp.zeros((row_count, width), jnp.float32)
    last = jnp.zeros((row_count, width), jnp.float32)
    for c in range(channels):
        cells = field_ref[c]
        here = lane == c
        first = jnp.where(here, cells if c == 0 else pltpu.roll(cells, c, 1), first)
        last = jnp.where(here, pltpu.roll(cells, c + 1, 1), last)
    first_ref[...] = first[:, :channels]
    last_ref[...] = last[:, :channels]


def edge_columns(field):
    channels, row_count, _ = field.shape
    shape = jax.ShapeDtypeStruct((row_count, channels), jnp.float32)
    return pl.pallas_call(
        edges_kernel, out_shape=(shape, shape), in_specs=[VMEM], out_specs=(VMEM, VMEM)
    )(field)


def step_kernel(rows, field_ref, east_ref, north_ref, up_ref, down_ref, west_col_ref, east_col_ref, out_ref):
    channels, row_count, width = field_ref.shape
    start, count = rows
    here = slice(start, start + count)
    lane = lax.broadcasted_iota(jnp.int32, (count, width), 1)
    row = lax.broadcasted_iota(jnp.int32, (count, width), 0)
    east, north = 0.5 * east_ref[here, :], 0.5 * north_ref[here, :]
    to_east, to_west = DIFFUSION - east, DIFFUSION + east
    to_south, to_north = DIFFUSION - north, DIFFUSION + north
    pad = jnp.zeros((count, width - channels), jnp.float32)
    west_col = jnp.concatenate([west_col_ref[here, :], pad], axis=1)
    east_col = jnp.concatenate([east_col_ref[here, :], pad], axis=1)
    for c in range(channels):
        cells = field_ref[c, here, :]
        west = jnp.where(lane == 0, pltpu.roll(west_col, (width - c) % width, 1), pltpu.roll(cells, 1, 1))
        east = jnp.where(
            lane == width - 1, pltpu.roll(east_col, width - 1 - c, 1), pltpu.roll(cells, width - 1, 1)
        )
        above = up_ref[c : c + 1, :] if start == 0 else field_ref[c, start - 1 : start, :]
        below = down_ref[c : c + 1, :] if start + count == row_count else field_ref[c, start + count : start + count + 1, :]
        up = jnp.where(row == 0, above, pltpu.roll(cells, 1, 0))
        down = jnp.where(row == count - 1, below, pltpu.roll(cells, count - 1, 0))
        stepped = (
            (1.0 - 4.0 * DIFFUSION) * cells + to_east * east + to_west * west + to_south * down + to_north * up
        )
        out_ref[c] = stepped.astype(out_ref.dtype)


def step(rows, dtype, field, *others):
    channels, _, width = field.shape
    return pl.pallas_call(
        functools.partial(step_kernel, rows),
        out_shape=jax.ShapeDtypeStruct((channels, rows[1], width), dtype),
        in_specs=[VMEM] * 7,
        out_specs=VMEM,
        compiler_params=pltpu.CompilerParams(vmem_limit_bytes=16 * 1024 * 1024),
        cost_estimate=pl.CostEstimate(flops=field.size * 9, bytes_accessed=field.size * 8, transcendentals=0),
    )(field, *others)


def on_device(lat_count, lon_count, atmosphere, east_speed, north_speed, owners, cutoff):
    channels, row_count, width = atmosphere.shape
    band = lax.axis_index("lat")
    mine = lax.axis_index("lon")
    bottom = band == lat_count - 1
    is_polar = jnp.logical_or(band == 0, bottom)
    even = band % 2 == 0
    flags = jnp.stack([bottom, band >= lat_count // 2, is_polar, (width - CAP * mine) % width]).astype(jnp.int32)

    exchange = functools.partial(lax.all_to_all, axis_name="lon", split_axis=0, concat_axis=0, tiled=True)
    sent = partial_step(flags, atmosphere, east_speed, north_speed)
    received = exchange(sent)
    owner_row = jnp.where(bottom, owners[1, :, 0], owners[0, :, 0])
    cut_row = jnp.where(bottom, cutoff[1], cutoff[0])
    same = owner_row[:, None] == owner_row[None, :]
    earlier = lax.iota(jnp.int32, row_count)[:, None] > lax.iota(jnp.int32, row_count)[None, :]
    rank = jnp.sum(jnp.logical_and(same, earlier).astype(jnp.int32), axis=1)
    slot = owner_row * CAP + rank

    def placed(values):
        blocks = values.reshape(row_count // 16, 16)
        return jnp.where(bottom, blocks[::-1], blocks).reshape(row_count, 1)

    def next_band(rows):
        pairs = [(lon_count + o, o) for o in range(lon_count)]
        pairs += [((lat_count - 2) * lon_count + o, (lat_count - 1) * lon_count + o) for o in range(lon_count)]
        return lax.ppermute(rows[:, row_count + 4], ("lat", "lon"), pairs)

    filtered = filter_rows(flags, received, next_band, placed(cut_row), placed(slot))
    returned = exchange(filtered)

    atmosphere, _ = lax.optimization_barrier((atmosphere, sent))
    first_col, last_col = edge_columns(atmosphere)
    west_col = lax.ppermute(last_col, "lon", [(o, (o + 1) % lon_count) for o in range(lon_count)])
    east_col = lax.ppermute(first_col, "lon", [((o + 1) % lon_count, o) for o in range(lon_count)])
    first_row, last_row = atmosphere[:, 0], atmosphere[:, -1]
    up = lax.ppermute(last_row, "lat", [(b, b + 1) for b in range(lat_count - 1)])
    down = lax.ppermute(first_row, "lat", [(b + 1, b) for b in range(lat_count - 1)])
    full = step((0, row_count), jnp.float32, atmosphere, east_speed, north_speed, up, down, west_col, east_col)
    return merge(flags, returned, full)


def solution(mesh):
    in_specs = (P(None, "lat", "lon"), P("lat", "lon"), P("lat", "lon"), P(), P())
    out_specs = (P(None, "lat", "lon"), P("lat", "lon"))
    return jax.shard_map(
        functools.partial(on_device, mesh.shape["lat"], mesh.shape["lon"]),
        mesh=mesh,
        in_specs=in_specs,
        out_specs=out_specs,
        check_vma=False,
    )
```

```python
import functools
import math

import jax
import jax.numpy as jnp
import ml_dtypes
import numpy as np
from jax import lax
from jax.experimental import pallas as pl
from jax.experimental.pallas import tpu as pltpu
from jax.sharding import PartitionSpec as P

LEV = 8
DIFFUSION = 0.1
CAP = 4
EXTRA = 8
VMEM = pl.BlockSpec(memory_space=pltpu.VMEM)


def real_forward(values):
    n = len(values)
    if n == 1:
        return [(values[0], None)]
    even = real_forward(values[0::2])
    odd = real_forward(values[1::2])
    half = n // 2
    out = [None] * (half + 1)
    for k in range(half // 2 + 1):
        er, ei = even[k]
        orr, oi = odd[k]
        if k == 0:
            out[0] = (er + orr, None)
            out[half] = (er - orr, None)
        elif 2 * k == half:
            out[k] = (er, -orr)
        else:
            c, s = math.cos(2 * math.pi * k / n), math.sin(2 * math.pi * k / n)
            if 8 * k == n:
                tr, ti = (orr + oi) * c, (oi - orr) * c
            else:
                tr, ti = orr * c + oi * s, oi * c - orr * s
            out[k] = (er + tr, ei + ti)
            out[half - k] = (er - tr, ti - ei)
    return out


def real_inverse(coefs):
    half = len(coefs) - 1
    if half == 0:
        return [coefs[0][0]]
    n = 2 * half
    even, odd = [None] * (half // 2 + 1), [None] * (half // 2 + 1)
    for k in range(half // 2 + 1):
        ar, ai = coefs[k]
        br, bi = coefs[half - k]
        if k == 0:
            even[0], odd[0] = (ar + br, None), (ar - br, None)
        elif 2 * k == half:
            even[k], odd[k] = (ar + ar, None), (-(ai + ai), None)
        else:
            even[k] = (ar + br, ai - bi)
            dr, di = ar - br, ai + bi
            c, s = math.cos(2 * math.pi * k / n), math.sin(2 * math.pi * k / n)
            if 8 * k == n:
                odd[k] = ((dr - di) * c, (dr + di) * c)
            else:
                odd[k] = (dr * c - di * s, di * c + dr * s)
    if half == 1:
        return [even[0][0], odd[0][0]]
    first, second = real_inverse(even), real_inverse(odd)
    return [v for pair in zip(first, second) for v in pair]


@functools.lru_cache(None)
def tables(parts, width):
    length = parts * width
    steps = np.arange(width)[:, None] * np.arange(width)[None, :] % width
    angle = 2 * np.pi * steps / width
    cos, sin = np.cos(angle), np.sin(angle)
    forward = np.block([[cos, -sin], [sin, cos]])
    inverse = forward.T / length

    def halves(table):
        high = table.astype(ml_dtypes.bfloat16)
        low = (table - high.astype(np.float64)).astype(ml_dtypes.bfloat16)
        return np.stack([high, low])

    turn = 2 * np.pi * np.arange(parts // 2 + 1)[:, None] * np.arange(width)[None, :] / length
    twiddle = np.stack([np.cos(turn), np.sin(turn)]).astype(np.float32)
    return np.stack([halves(forward), halves(inverse)]), twiddle


def split_halves(value):
    high = value.astype(jnp.bfloat16)
    return high, (value - high.astype(jnp.float32)).astype(jnp.bfloat16)


def add_edges(values, edge, lane):
    width, parts = lane.shape[1], len(values)
    rim = jnp.logical_or(lane == 0, lane == width - 1)
    return [
        value + jnp.where(rim, pltpu.roll(edge, (width - 2 * (parts - 1 - s) - 1) % width, 1), 0.0)
        for s, value in enumerate(values)
    ]


def at_bottom():
    return lax.axis_index("lat") == lax.axis_size("lat") - 1


def filter_kernel(parts, first_block, block_count, rows_ref, *refs):
    last_call = first_block > 0
    if last_call:
        halo_ref, cut_ref, slot_ref, mat_ref, tw_ref, edge_ref, before_ref, _, out_ref, *refs = refs
    else:
        cut_ref, slot_ref, mat_ref, tw_ref, out_ref, edge_ref, energy_ref, *refs = refs
    extra_ref, pair_ref, high_ref, low_ref, wave_ref, done_ref, sems = refs
    count = parts // 2 + 1
    row_count, width = rows_ref.shape[1] - EXTRA, rows_ref.shape[2]
    bottom = at_bottom()
    rows_here = 16 * block_count

    for i in range(parts):
        extra_ref[i * EXTRA : (i + 1) * EXTRA, :] = rows_ref[i, row_count : row_count + EXTRA, :].astype(jnp.float32)

    def extra(i):
        return extra_ref[pl.ds(i, parts, stride=EXTRA), :]

    if last_call:
        border = extra(5) * halo_ref[...].astype(jnp.float32)
        border_row = jnp.where(bottom, 0, 15)
    else:
        turned = pltpu.roll(extra(0), width // 2, 1)
        coef = extra(1)
        from_west = coef * pltpu.roll(turned, parts - 1, 0)
        from_east = pltpu.roll(coef * pltpu.roll(turned, 1, 0), width // 2, 1)
        pair_ref[pl.ds(0, parts, stride=2), :] = from_east
        pair_ref[pl.ds(1, parts, stride=2), :] = from_west
        edge = pair_ref[...].T[:row_count, :]
        edge_ref[...] = jnp.concatenate([edge, jnp.zeros((row_count, width - 2 * parts), jnp.float32)], axis=1)
        border = extra(3) * pltpu.roll(extra(2), parts // 2, 0)
        border_row = jnp.where(bottom, 15, 0)
    lane = lax.broadcasted_iota(jnp.int32, (8, width), 1)
    sub = lax.broadcasted_iota(jnp.int32, (8, width), 0)

    for block in range(block_count):
        at = slice(16 * block, 16 * block + 16)
        source = first_block + block
        natural = jnp.where(bottom, 48 - 16 * source, 16 * source)
        has_border = source == (3 if last_call else 0)
        halves = []
        for part in range(2):
            values = [
                rows_ref[parts - 1 - s, 16 * source : 16 * source + 16, :].astype(jnp.float32)[part * 8 : part * 8 + 8]
                for s in range(parts)
            ]
            values = add_edges(values, edge_ref[pl.ds(pl.multiple_of(natural + 8 * part, 8), 8), :], lane)
            if has_border:
                here = sub + 8 * part == border_row
                values = [
                    v + jnp.where(here, border[parts - 1 - s : parts - s, :], 0.0) for s, v in enumerate(values)
                ]
            spun = []
            for k, (re, im) in enumerate(real_forward(values)):
                if k == 0:
                    spun.append((re, jnp.zeros_like(re)))
                    continue
                c, sn = tw_ref[0, k : k + 1, :], tw_ref[1, k : k + 1, :]
                if im is None:
                    spun.append((re * c, -(re * sn)))
                else:
                    spun.append((re * c + im * sn, im * c - re * sn))
            halves.append(spun)
        for k in range(count):
            for side in range(2):
                value = jnp.concatenate([halves[0][k][side], halves[1][k][side]], axis=0)
                high, low = split_halves(value)
                lanes = slice(side * width, (side + 1) * width)
                high_ref[k, at, lanes] = high
                low_ref[k, at, lanes] = low

    cut = cut_ref[16 * first_block : 16 * first_block + rows_here, :]
    wide = lax.broadcasted_iota(jnp.int32, (rows_here, width), 1)
    wide = jnp.concatenate([wide, wide], axis=1)
    dot = functools.partial(jnp.dot, preferred_element_type=jnp.float32)
    step = 6 if block_count > 1 else count
    for k0 in range(0, count, step):
        k1 = min(count, k0 + step)
        flat = ((k1 - k0) * rows_here, 2 * width)
        high, low = high_ref[k0:k1].reshape(flat), low_ref[k0:k1].reshape(flat)
        coef = dot(high, mat_ref[0, 0]) + dot(low, mat_ref[0, 0]) + dot(high, mat_ref[0, 1])
        kept = []
        for k in range(k0, k1):
            wave = k + parts * wide
            keep = jnp.minimum(wave, parts * width - wave) < cut
            kept.append(jnp.where(keep, coef[(k - k0) * rows_here : (k - k0 + 1) * rows_here], 0.0))
        high, low = split_halves(jnp.concatenate(kept, axis=0))
        wave = dot(high, mat_ref[1, 0]) + dot(low, mat_ref[1, 0]) + dot(high, mat_ref[1, 1])
        wave_ref[k0:k1] = wave.reshape(k1 - k0, rows_here, 2 * width)

    copies = []
    energy = before_ref[...] if last_call else jnp.zeros((8, width), jnp.float32)
    for block in range(block_count):
        source = first_block + block
        halves = []
        for part in range(2):
            here = slice(16 * block + 8 * part, 16 * block + 8 * part + 8)
            coefs = []
            for k in range(count):
                re, im = wave_ref[k, here, :width], wave_ref[k, here, width:]
                if k == 0:
                    coefs.append((re, None))
                    continue
                c, sn = tw_ref[0, k : k + 1, :], tw_ref[1, k : k + 1, :]
                coefs.append((re * c - im * sn, None if 2 * k == parts else im * c + re * sn))
            values = real_inverse(coefs)
            total = values[0] * values[0]
            for value in values[1:]:
                total = total + value * value
            row_sum = jnp.sum(total, axis=1, keepdims=True)
            slots = slot_ref[16 * source + 8 * part : 16 * source + 8 * part + 8, :]
            energy = energy + jnp.where(slots == lane, row_sum, 0.0)
            halves.append(values)
        for s in range(parts):
            done_ref[parts - 1 - s, 16 * block : 16 * block + 16, :] = jnp.concatenate(
                [halves[0][s], halves[1][s]], axis=0
            ).astype(jnp.bfloat16)
        if not last_call:
            copies.append(
                pltpu.make_async_copy(
                    done_ref.at[:, pl.ds(16 * block, 16)], out_ref.at[:, pl.ds(16 * source, 16)], sems.at[block]
                )
            )
            copies[-1].start()
    if last_call:
        total = jnp.sum(energy, axis=0, keepdims=True)
        high = total.astype(jnp.bfloat16).astype(jnp.float32)
        tail = jnp.where(sub == 0, high, jnp.where(sub == 1, total - high, 0.0)).astype(jnp.bfloat16)
        for s in range(parts):
            done_ref[s, rows_here : rows_here + EXTRA, :] = tail
        copies.append(
            pltpu.make_async_copy(done_ref, out_ref.at[:, pl.ds(16 * first_block, rows_here + EXTRA)], sems.at[0])
        )
        copies[-1].start()
    else:
        energy_ref[...] = energy
    for copy in copies:
        copy.wait()


def filter_rows(rows, halo, cut, slot):
    parts, row_count, width = rows.shape
    row_count -= EXTRA
    count = parts // 2 + 1
    mats, twiddle = tables(parts, width)
    operands = (cut, slot, jnp.asarray(mats), jnp.asarray(twiddle))
    anywhere = pl.BlockSpec(memory_space=pl.ANY)

    def call(first_block, block_count, out_shape, out_specs, aliases, last_spec, *args):
        rows_here = 16 * block_count
        tail = EXTRA if first_block else 0
        return pl.pallas_call(
            functools.partial(filter_kernel, parts, first_block, block_count),
            out_shape=out_shape,
            in_specs=[VMEM] * (len(args) - 1) + [last_spec],
            out_specs=out_specs,
            input_output_aliases=aliases,
            scratch_shapes=[
                pltpu.VMEM((parts * EXTRA, width), jnp.float32),
                pltpu.VMEM((2 * parts, width), jnp.float32),
                pltpu.VMEM((count, rows_here, 2 * width), jnp.bfloat16),
                pltpu.VMEM((count, rows_here, 2 * width), jnp.bfloat16),
                pltpu.VMEM((count, rows_here, 2 * width), jnp.float32),
                pltpu.VMEM((parts, rows_here + tail, width), jnp.bfloat16),
                pltpu.SemaphoreType.DMA((block_count,)),
            ],
            compiler_params=pltpu.CompilerParams(vmem_limit_bytes=24 * 1024 * 1024),
            cost_estimate=pl.CostEstimate(
                flops=rows_here * parts * width * 8000, bytes_accessed=rows.size * 4, transcendentals=0
            ),
        )(*args)

    whole = jax.ShapeDtypeStruct(rows.shape, jnp.bfloat16)
    edge = jax.ShapeDtypeStruct((row_count, width), jnp.float32)
    energy = jax.ShapeDtypeStruct((8, width), jnp.float32)
    halo_rows = halo(rows)
    out, edge, energy = call(
        0, 3, (whole, edge, energy), (anywhere, VMEM, VMEM), {}, VMEM, rows, *operands
    )
    args = (rows, halo_rows, *operands, edge, energy, out)
    return call(3, 1, whole, anywhere, {len(args) - 1: 0}, anywhere, *args)


GROUP = 8


def brought(field_ref, flat_refs, field, flats, in_sems):
    flat_copies = [
        pltpu.make_async_copy(ref, flats.at[i], in_sems.at[i]) for i, ref in enumerate(flat_refs)
    ]
    copies = []
    for g in range(field.shape[0] // GROUP):
        here = pl.ds(g * GROUP, GROUP)
        copies.append(pltpu.make_async_copy(field_ref.at[here], field.at[here], in_sems.at[len(flat_refs) + g]))
    for copy in copies[:1] + flat_copies + copies[1:]:
        copy.start()
    return flat_copies, copies


def partial_kernel(
    field_any, east_any, north_any, out_any, cols_any, rows_any,
    field_ref, flat_ref, out_ref, cols_ref, rows_ref, acc_ref, in_sems, out_sems,
):
    channels, row_count, width = field_ref.shape
    flat_copies, copies = brought(field_any, (east_any, north_any), field_ref, flat_ref, in_sems)
    lane = lax.broadcasted_iota(jnp.int32, (row_count, width), 1)
    row = lax.broadcasted_iota(jnp.int32, (row_count, width), 0)
    sub = lax.broadcasted_iota(jnp.int32, (EXTRA, width), 0)
    bottom = at_bottom()
    lower = lax.axis_index("lat") >= lax.axis_size("lat") // 2
    for copy in flat_copies:
        copy.wait()
    east, north = 0.5 * flat_ref[0], 0.5 * flat_ref[1]
    to_east, to_west = DIFFUSION - east, DIFFUSION + east
    to_south, to_north = DIFFUSION - north, DIFFUSION + north
    mid_east = jnp.where(lane == width - 1, 0.0, to_east)
    mid_west = jnp.where(lane == 0, 0.0, to_west)
    mid_south = jnp.where(row == row_count - 1, 0.0, to_south)
    mid_north = jnp.where(row == 0, 0.0, to_north)
    outer = jnp.where(bottom, to_south[row_count - 1 :, :], to_north[:1, :])
    inner = jnp.where(bottom, to_north[:1, :], to_south[row_count - 1 :, :])
    shift = 2 * GROUP + 1
    rim = jnp.where(lane == shift, pltpu.roll(to_west, shift, 1), 0.0)
    rim = jnp.where(lane == shift - 1, pltpu.roll(to_east, shift, 1), rim)
    sent = []
    for g, copy in enumerate(copies):
        copy.wait()
        acc = rim
        for i in range(GROUP):
            c = g * GROUP + i
            cells = field_ref[c]
            here = jnp.logical_or(lane == 2 * i, lane == 2 * i + 1)
            acc = jnp.where(here, pltpu.roll(cells, 2 * i + 1, 1), acc)
            stepped = (
                (1.0 - 4.0 * DIFFUSION) * cells
                + mid_east * pltpu.roll(cells, width - 1, 1)
                + mid_west * pltpu.roll(cells, 1, 1)
                + mid_south * pltpu.roll(cells, row_count - 1, 0)
                + mid_north * pltpu.roll(cells, 1, 0)
            ).astype(jnp.bfloat16)
            for t in range(row_count // 16):
                at = jnp.where(bottom, row_count - 16 - 16 * t, 16 * t)
                out_ref[c, pl.ds(pl.multiple_of(at, 16), 16), :] = stepped[16 * t : 16 * t + 16]
        acc_ref[g] = acc.T
        last = acc_ref[g, pl.ds(0, GROUP, stride=2), :]
        first = acc_ref[g, pl.ds(1, GROUP, stride=2), :]
        edges = jnp.concatenate([first, last], axis=1)
        rims = jnp.concatenate([acc_ref[g, shift : shift + 1, :], acc_ref[g, shift - 1 : shift, :]], axis=1)
        cols_ref[0, g * GROUP : (g + 1) * GROUP, :] = first
        cols_ref[1, g * GROUP : (g + 1) * GROUP, :] = last
        for i in range(GROUP):
            c = g * GROUP + i
            top_row, low_row = field_ref[c, 0:1, :], field_ref[c, row_count - 1 : row_count, :]
            rows_ref[0, c : c + 1, :] = top_row
            rows_ref[1, c : c + 1, :] = low_row
            tail = jnp.where(sub == 0, edges[i : i + 1, :], 0.0)
            tail = jnp.where(sub == 1, rims, tail)
            tail = jnp.where(sub == 2, jnp.where(bottom, low_row, top_row), tail)
            tail = jnp.where(sub == 3, -outer if c < 2 * LEV else outer, tail)
            tail = jnp.where(sub == 4, jnp.where(lower, low_row, top_row), tail)
            tail = jnp.where(sub == 5, inner, tail)
            out_ref[c, row_count : row_count + EXTRA, :] = tail.astype(jnp.bfloat16)
        here = pl.ds(g * GROUP, GROUP)
        sent.append(pltpu.make_async_copy(out_ref.at[here], out_any.at[here], out_sems.at[g]))
        sent[-1].start()
    for i, (source, target) in enumerate(((cols_ref, cols_any), (rows_ref, rows_any))):
        sent.append(pltpu.make_async_copy(source, target, out_sems.at[len(copies) + i]))
        sent[-1].start()
    for copy in sent:
        copy.wait()


def partial_step(field, east_speed, north_speed):
    channels, row_count, width = field.shape
    anywhere = pl.BlockSpec(memory_space=pl.ANY)
    payload = (channels, row_count + EXTRA, width)
    cols, rows = (2, channels, row_count), (2, channels, width)
    return pl.pallas_call(
        partial_kernel,
        out_shape=(
            jax.ShapeDtypeStruct(payload, jnp.bfloat16),
            jax.ShapeDtypeStruct(cols, jnp.float32),
            jax.ShapeDtypeStruct(rows, jnp.float32),
        ),
        in_specs=[anywhere] * 3,
        out_specs=(anywhere, anywhere, anywhere),
        scratch_shapes=[
            pltpu.VMEM(field.shape, jnp.float32),
            pltpu.VMEM((2, row_count, width), jnp.float32),
            pltpu.VMEM(payload, jnp.bfloat16),
            pltpu.VMEM(cols, jnp.float32),
            pltpu.VMEM(rows, jnp.float32),
            pltpu.VMEM((channels // GROUP, width, row_count), jnp.float32),
            pltpu.SemaphoreType.DMA((channels // GROUP + 2,)),
            pltpu.SemaphoreType.DMA((channels // GROUP + 2,)),
        ],
        cost_estimate=pl.CostEstimate(flops=field.size * 9, bytes_accessed=field.size * 6, transcendentals=0),
    )(field, east_speed, north_speed)


def merge_kernel(back_ref, full_ref, out_ref, energy_ref, wide_ref, sems):
    del full_ref
    channels, row_count, width = out_ref.shape
    bottom = at_bottom()
    polar = jnp.logical_or(bottom, lax.axis_index("lat") == 0)
    shift = lax.rem(width - CAP * lax.axis_index("lon"), width)
    group = 8

    @pl.when(polar)
    def _():
        copies = []
        for g in range(channels // group):
            for c in range(g * group, (g + 1) * group):
                for t in range(row_count // 16):
                    at = jnp.where(bottom, row_count - 16 - 16 * t, 16 * t)
                    wide_ref[c, 16 * t : 16 * t + 16, :] = back_ref[
                        c, pl.ds(pl.multiple_of(at, 16), 16), :
                    ].astype(jnp.float32)
            here = pl.ds(g * group, group)
            copies.append(pltpu.make_async_copy(wide_ref.at[here], out_ref.at[here], sems.at[g]))
            copies[-1].start()
        total = jnp.zeros((EXTRA, width), jnp.float32)
        for c in range(channels):
            total = total + back_ref[c, row_count : row_count + EXTRA, :].astype(jnp.float32)
        energy = jnp.sum(total, axis=0, keepdims=True) * (1.0 / (channels * channels * width))
        energy = pltpu.roll(jnp.broadcast_to(energy, (8, width)), shift, 1)
        energy_ref[...] = energy[:1, :CAP]
        for copy in copies:
            copy.wait()

    @pl.when(jnp.logical_not(polar))
    def _():
        energy_ref[...] = jnp.zeros((1, CAP), jnp.float32)


def merge(back, full):
    channels, row_count, width = full.shape
    anywhere = pl.BlockSpec(memory_space=pl.ANY)
    return pl.pallas_call(
        merge_kernel,
        out_shape=(
            jax.ShapeDtypeStruct(full.shape, jnp.float32),
            jax.ShapeDtypeStruct((1, CAP), jnp.float32),
        ),
        in_specs=[VMEM, anywhere],
        out_specs=(anywhere, VMEM),
        input_output_aliases={1: 0},
        scratch_shapes=[pltpu.VMEM(full.shape, jnp.float32), pltpu.SemaphoreType.DMA((channels // 8,))],
        compiler_params=pltpu.CompilerParams(vmem_limit_bytes=16 * 1024 * 1024),
    )(back, full)


def step_kernel(
    field_any, east_any, north_any, up_ref, down_ref, west_col_ref, east_col_ref, out_any,
    field_ref, flat_ref, out_ref, col_ref, in_sems, out_sems,
):
    channels, row_count, width = field_ref.shape
    flat_copies, copies = brought(field_any, (east_any, north_any), field_ref, flat_ref, in_sems)
    lane = lax.broadcasted_iota(jnp.int32, (row_count, width), 1)
    row = lax.broadcasted_iota(jnp.int32, (row_count, width), 0)
    col_ref[pl.ds(0, channels, stride=2), :row_count] = east_col_ref[...]
    col_ref[pl.ds(1, channels, stride=2), :row_count] = west_col_ref[...]
    cols = col_ref[...].T[:row_count, :]
    cols = jnp.concatenate([cols, jnp.zeros((row_count, width - 2 * channels), jnp.float32)], axis=1)
    for copy in flat_copies:
        copy.wait()
    east, north = 0.5 * flat_ref[0], 0.5 * flat_ref[1]
    to_east, to_west = DIFFUSION - east, DIFFUSION + east
    to_south, to_north = DIFFUSION - north, DIFFUSION + north
    sent = []
    for g, copy in enumerate(copies):
        copy.wait()
        for c in range(g * GROUP, (g + 1) * GROUP):
            cells = field_ref[c]
            rim = pltpu.roll(cols, (width - 2 * c - 1) % width, 1)
            west = jnp.where(lane == 0, rim, pltpu.roll(cells, 1, 1))
            east = jnp.where(lane == width - 1, rim, pltpu.roll(cells, width - 1, 1))
            up = jnp.where(row == 0, up_ref[c : c + 1, :], pltpu.roll(cells, 1, 0))
            down = jnp.where(row == row_count - 1, down_ref[c : c + 1, :], pltpu.roll(cells, row_count - 1, 0))
            out_ref[c] = (
                (1.0 - 4.0 * DIFFUSION) * cells + to_east * east + to_west * west + to_south * down + to_north * up
            )
        here = pl.ds(g * GROUP, GROUP)
        sent.append(pltpu.make_async_copy(out_ref.at[here], out_any.at[here], out_sems.at[g]))
        sent[-1].start()
    for copy in sent:
        copy.wait()


def step(field, east_speed, north_speed, up, down, west_col, east_col):
    channels, row_count, width = field.shape
    anywhere = pl.BlockSpec(memory_space=pl.ANY)
    return pl.pallas_call(
        step_kernel,
        out_shape=jax.ShapeDtypeStruct(field.shape, jnp.float32),
        in_specs=[anywhere] * 3 + [VMEM] * 4,
        out_specs=anywhere,
        scratch_shapes=[
            pltpu.VMEM(field.shape, jnp.float32),
            pltpu.VMEM((2, row_count, width), jnp.float32),
            pltpu.VMEM(field.shape, jnp.float32),
            pltpu.VMEM((2 * channels, width), jnp.float32),
            pltpu.SemaphoreType.DMA((channels // GROUP + 2,)),
            pltpu.SemaphoreType.DMA((channels // GROUP,)),
        ],
        cost_estimate=pl.CostEstimate(flops=field.size * 9, bytes_accessed=field.size * 8, transcendentals=0),
    )(field, east_speed, north_speed, up, down, west_col, east_col)


def on_device(lat_count, lon_count, atmosphere, east_speed, north_speed, owners, cutoff):
    channels, row_count, width = atmosphere.shape
    bottom = at_bottom()

    groups = [list(range(lon_count))[::-1]]
    exchange = functools.partial(
        lax.all_to_all, axis_name="lon", split_axis=0, concat_axis=0, tiled=True, axis_index_groups=groups
    )
    sent, cols, edge_rows = partial_step(atmosphere, east_speed, north_speed)
    received = exchange(sent)
    owner_row = jnp.where(bottom, owners[1, :, 0], owners[0, :, 0])
    cut_row = jnp.where(bottom, cutoff[1], cutoff[0])
    same = owner_row[:, None] == owner_row[None, :]
    earlier = lax.iota(jnp.int32, row_count)[:, None] > lax.iota(jnp.int32, row_count)[None, :]
    rank = jnp.sum(jnp.logical_and(same, earlier).astype(jnp.int32), axis=1)
    slot = owner_row * CAP + rank

    def placed(values):
        blocks = values.reshape(row_count // 16, 16)
        return jnp.where(bottom, blocks[::-1], blocks).reshape(row_count, 1)

    def next_band(rows):
        pairs = [(b * lon_count + o, (b ^ 1) * lon_count + o) for b in range(lat_count) for o in range(lon_count)]
        return lax.ppermute(rows[:, row_count + 4], ("lat", "lon"), pairs)

    west_col = lax.ppermute(cols[1], "lon", [(o, (o + 1) % lon_count) for o in range(lon_count)])
    east_col = lax.ppermute(cols[0], "lon", [((o + 1) % lon_count, o) for o in range(lon_count)])
    up = lax.ppermute(edge_rows[1], "lat", [(b, b + 1) for b in range(lat_count - 1)])
    down = lax.ppermute(edge_rows[0], "lat", [(b + 1, b) for b in range(lat_count - 1)])
    received, halos = lax.optimization_barrier((received, (up, down, west_col, east_col)))
    filtered = filter_rows(received, next_band, placed(cut_row), placed(slot))
    returned = exchange(filtered)
    full = step(atmosphere, east_speed, north_speed, *halos)
    return merge(returned, full)


def solution(mesh):
    in_specs = (P(None, "lat", "lon"), P("lat", "lon"), P("lat", "lon"), P(), P())
    out_specs = (P(None, "lat", "lon"), P("lat", "lon"))
    return jax.shard_map(
        functools.partial(on_device, mesh.shape["lat"], mesh.shape["lon"]),
        mesh=mesh,
        in_specs=in_specs,
        out_specs=out_specs,
        check_vma=False,
    )
```

```python
import functools
import math

import jax
import jax.numpy as jnp
import ml_dtypes
import numpy as np
from jax import lax
from jax.experimental import pallas as pl
from jax.experimental.pallas import tpu as pltpu
from jax.sharding import PartitionSpec as P

LEV = 8
DIFFUSION = 0.1
CAP = 4
EXTRA = 8
VMEM = pl.BlockSpec(memory_space=pltpu.VMEM)


def real_forward(values):
    n = len(values)
    if n == 1:
        return [(values[0], None)]
    even = real_forward(values[0::2])
    odd = real_forward(values[1::2])
    half = n // 2
    out = [None] * (half + 1)
    for k in range(half // 2 + 1):
        er, ei = even[k]
        orr, oi = odd[k]
        if k == 0:
            out[0] = (er + orr, None)
            out[half] = (er - orr, None)
        elif 2 * k == half:
            out[k] = (er, -orr)
        else:
            c, s = math.cos(2 * math.pi * k / n), math.sin(2 * math.pi * k / n)
            if 8 * k == n:
                tr, ti = (orr + oi) * c, (oi - orr) * c
            else:
                tr, ti = orr * c + oi * s, oi * c - orr * s
            out[k] = (er + tr, ei + ti)
            out[half - k] = (er - tr, ti - ei)
    return out


def real_inverse(coefs):
    half = len(coefs) - 1
    if half == 0:
        return [coefs[0][0]]
    n = 2 * half
    even, odd = [None] * (half // 2 + 1), [None] * (half // 2 + 1)
    for k in range(half // 2 + 1):
        ar, ai = coefs[k]
        br, bi = coefs[half - k]
        if k == 0:
            even[0], odd[0] = (ar + br, None), (ar - br, None)
        elif 2 * k == half:
            even[k], odd[k] = (ar + ar, None), (-(ai + ai), None)
        else:
            even[k] = (ar + br, ai - bi)
            dr, di = ar - br, ai + bi
            c, s = math.cos(2 * math.pi * k / n), math.sin(2 * math.pi * k / n)
            if 8 * k == n:
                odd[k] = ((dr - di) * c, (dr + di) * c)
            else:
                odd[k] = (dr * c - di * s, di * c + dr * s)
    if half == 1:
        return [even[0][0], odd[0][0]]
    first, second = real_inverse(even), real_inverse(odd)
    return [v for pair in zip(first, second) for v in pair]


@functools.lru_cache(None)
def tables(parts, width):
    length = parts * width
    steps = np.arange(width)[:, None] * np.arange(width)[None, :] % width
    angle = 2 * np.pi * steps / width
    cos, sin = np.cos(angle), np.sin(angle)
    forward = np.block([[cos, -sin], [sin, cos]])
    inverse = forward.T / length

    def halves(table):
        high = table.astype(ml_dtypes.bfloat16)
        low = (table - high.astype(np.float64)).astype(ml_dtypes.bfloat16)
        return np.stack([high, low])

    turn = 2 * np.pi * np.arange(parts // 2 + 1)[:, None] * np.arange(width)[None, :] / length
    twiddle = np.stack([np.cos(turn), np.sin(turn)]).astype(np.float32)
    return np.stack([halves(forward), halves(inverse)]), twiddle


def split_halves(value):
    high = value.astype(jnp.bfloat16)
    return high, (value - high.astype(jnp.float32)).astype(jnp.bfloat16)


def add_edges(values, edge, lane):
    width = lane.shape[1]
    rim = jnp.logical_or(lane == 0, lane == width - 1)
    return [
        value + jnp.where(rim, pltpu.roll(edge, (width - 2 * s - 1) % width, 1), 0.0)
        for s, value in enumerate(values)
    ]


def rank_order(parts):
    half, quarter = parts // 2, parts // 4
    return [*range(parts - 1, half - 1, -1), *range(quarter - 1, -1, -1), *range(half - 1, quarter - 1, -1)]


def at_bottom():
    return lax.axis_index("lat") == lax.axis_size("lat") - 1


def filter_kernel(parts, first_block, block_count, rows_ref, *refs):
    order = rank_order(parts)
    place = [order.index(s) for s in range(parts)]
    last_call = first_block > 0
    if last_call:
        halo_ref, cut_ref, slot_ref, mat_ref, tw_ref, edge_ref, before_ref, earlier_ref, out_ref, *refs = refs
    else:
        cut_ref, slot_ref, mat_ref, tw_ref, done_ref, edge_ref, energy_ref, *refs = refs
    extra_ref, pair_ref, high_ref, low_ref, wave_ref, *refs = refs
    count = parts // 2 + 1
    row_count, width = rows_ref.shape[1] - EXTRA, rows_ref.shape[2]
    bottom = at_bottom()
    rows_here = 16 * block_count
    if last_call:
        done_ref, sems = refs
        copies = [pltpu.make_async_copy(earlier_ref, out_ref.at[:, pl.ds(0, 16 * first_block)], sems.at[0])]
        copies[0].start()

    for i in range(parts):
        extra_ref[order[i] * EXTRA : (order[i] + 1) * EXTRA, :] = rows_ref[i, row_count : row_count + EXTRA, :].astype(jnp.float32)

    def extra(i):
        return extra_ref[pl.ds(i, parts, stride=EXTRA), :]

    if last_call:
        halo = halo_ref[...].astype(jnp.float32)
        for i in range(parts):
            pair_ref[order[i] : order[i] + 1, :] = halo[i : i + 1, :]
        border = extra(6) * pair_ref[:parts, :]
        border_row = jnp.where(bottom, 0, 15)
    else:
        odd = lax.axis_index("lon") % 2 == 0
        first, last = (jnp.where(odd, pltpu.roll(extra(i), width // 2, 1), extra(i)) for i in range(2))
        coef = extra(2)
        from_west = coef * pltpu.roll(last, 1, 0)
        from_east = pltpu.roll(coef, width // 2, 1) * pltpu.roll(first, parts - 1, 0)
        pair_ref[pl.ds(0, parts, stride=2), :] = from_east
        pair_ref[pl.ds(1, parts, stride=2), :] = from_west
        edge = pair_ref[...].T[:row_count, :]
        edge_ref[...] = jnp.concatenate([edge, jnp.zeros((row_count, width - 2 * parts), jnp.float32)], axis=1)
        border = extra(4) * pltpu.roll(extra(3), parts // 2, 0)
        border_row = jnp.where(bottom, 15, 0)
    lane = lax.broadcasted_iota(jnp.int32, (8, width), 1)
    sub = lax.broadcasted_iota(jnp.int32, (8, width), 0)

    for block in range(block_count):
        at = slice(16 * block, 16 * block + 16)
        source = first_block + block
        natural = jnp.where(bottom, 48 - 16 * source, 16 * source)
        has_border = source == (3 if last_call else 0)
        halves = []
        for part in range(2):
            values = [
                rows_ref[place[s], 16 * source : 16 * source + 16, :].astype(jnp.float32)[part * 8 : part * 8 + 8]
                for s in range(parts)
            ]
            values = add_edges(values, edge_ref[pl.ds(pl.multiple_of(natural + 8 * part, 8), 8), :], lane)
            if has_border:
                here = sub + 8 * part == border_row
                values = [
                    v + jnp.where(here, border[s : s + 1, :], 0.0) for s, v in enumerate(values)
                ]
            spun = []
            for k, (re, im) in enumerate(real_forward(values)):
                if k == 0:
                    spun.append((re, jnp.zeros_like(re)))
                    continue
                c, sn = tw_ref[0, k : k + 1, :], tw_ref[1, k : k + 1, :]
                if im is None:
                    spun.append((re * c, -(re * sn)))
                else:
                    spun.append((re * c + im * sn, im * c - re * sn))
            halves.append(spun)
        for k in range(count):
            for side in range(2):
                value = jnp.concatenate([halves[0][k][side], halves[1][k][side]], axis=0)
                high, low = split_halves(value)
                lanes = slice(side * width, (side + 1) * width)
                high_ref[k, at, lanes] = high
                low_ref[k, at, lanes] = low

    cut = cut_ref[16 * first_block : 16 * first_block + rows_here, :]
    wide = lax.broadcasted_iota(jnp.int32, (rows_here, width), 1)
    wide = jnp.concatenate([wide, wide], axis=1)
    dot = functools.partial(jnp.dot, preferred_element_type=jnp.float32)
    step = 6 if block_count > 1 else count
    for k0 in range(0, count, step):
        k1 = min(count, k0 + step)
        flat = ((k1 - k0) * rows_here, 2 * width)
        high, low = high_ref[k0:k1].reshape(flat), low_ref[k0:k1].reshape(flat)
        coef = dot(high, mat_ref[0, 0]) + dot(low, mat_ref[0, 0]) + dot(high, mat_ref[0, 1])
        kept = []
        for k in range(k0, k1):
            wave = k + parts * wide
            keep = jnp.minimum(wave, parts * width - wave) < cut
            kept.append(jnp.where(keep, coef[(k - k0) * rows_here : (k - k0 + 1) * rows_here], 0.0))
        high, low = split_halves(jnp.concatenate(kept, axis=0))
        wave = dot(high, mat_ref[1, 0]) + dot(low, mat_ref[1, 0]) + dot(high, mat_ref[1, 1])
        wave_ref[k0:k1] = wave.reshape(k1 - k0, rows_here, 2 * width)

    energy = before_ref[...] if last_call else jnp.zeros((8, width), jnp.float32)
    for block in range(block_count):
        source = first_block + block
        halves = []
        for part in range(2):
            here = slice(16 * block + 8 * part, 16 * block + 8 * part + 8)
            coefs = []
            for k in range(count):
                re, im = wave_ref[k, here, :width], wave_ref[k, here, width:]
                if k == 0:
                    coefs.append((re, None))
                    continue
                c, sn = tw_ref[0, k : k + 1, :], tw_ref[1, k : k + 1, :]
                coefs.append((re * c - im * sn, None if 2 * k == parts else im * c + re * sn))
            values = real_inverse(coefs)
            total = values[0] * values[0]
            for value in values[1:]:
                total = total + value * value
            row_sum = jnp.sum(total, axis=1, keepdims=True)
            slots = slot_ref[16 * source + 8 * part : 16 * source + 8 * part + 8, :]
            energy = energy + jnp.where(slots == lane, row_sum, 0.0)
            halves.append(values)
        for s in range(parts):
            done_ref[place[s], 16 * block : 16 * block + 16, :] = jnp.concatenate(
                [halves[0][s], halves[1][s]], axis=0
            ).astype(jnp.bfloat16)
    if last_call:
        total = jnp.sum(energy, axis=0, keepdims=True)
        high = total.astype(jnp.bfloat16).astype(jnp.float32)
        tail = jnp.where(sub == 0, high, jnp.where(sub == 1, total - high, 0.0)).astype(jnp.bfloat16)
        for s in range(parts):
            done_ref[s, rows_here : rows_here + EXTRA, :] = tail
        copies.append(
            pltpu.make_async_copy(done_ref, out_ref.at[:, pl.ds(16 * first_block, rows_here + EXTRA)], sems.at[1])
        )
        copies[-1].start()
        for copy in copies:
            copy.wait()
    else:
        energy_ref[...] = energy


def filter_rows(rows, halo, cut, slot):
    parts, row_count, width = rows.shape
    row_count -= EXTRA
    count = parts // 2 + 1
    mats, twiddle = tables(parts, width)
    operands = (cut, slot, jnp.asarray(mats), jnp.asarray(twiddle))
    anywhere = pl.BlockSpec(memory_space=pl.ANY)

    def call(first_block, block_count, out_shape, out_specs, own, *args):
        rows_here = 16 * block_count
        return pl.pallas_call(
            functools.partial(filter_kernel, parts, first_block, block_count),
            out_shape=out_shape,
            in_specs=[VMEM] * len(args),
            out_specs=out_specs,
            scratch_shapes=[
                pltpu.VMEM((parts * EXTRA, width), jnp.float32),
                pltpu.VMEM((2 * parts, width), jnp.float32),
                pltpu.VMEM((count, rows_here, 2 * width), jnp.bfloat16),
                pltpu.VMEM((count, rows_here, 2 * width), jnp.bfloat16),
                pltpu.VMEM((count, rows_here, 2 * width), jnp.float32),
                *own,
            ],
            compiler_params=pltpu.CompilerParams(vmem_limit_bytes=24 * 1024 * 1024),
            cost_estimate=pl.CostEstimate(
                flops=rows_here * parts * width * 8000, bytes_accessed=rows.size * 4, transcendentals=0
            ),
        )(*args)

    earlier = jax.ShapeDtypeStruct((parts, row_count - 16, width), jnp.bfloat16)
    whole = jax.ShapeDtypeStruct(rows.shape, jnp.bfloat16)
    edge = jax.ShapeDtypeStruct((row_count, width), jnp.float32)
    energy = jax.ShapeDtypeStruct((8, width), jnp.float32)
    halo_rows = halo(rows)
    first, edge, energy = call(0, 3, (earlier, edge, energy), (VMEM, VMEM, VMEM), [], rows, *operands)
    own = [pltpu.VMEM((parts, 16 + EXTRA, width), jnp.bfloat16), pltpu.SemaphoreType.DMA((2,))]
    return call(3, 1, whole, anywhere, own, rows, halo_rows, *operands, edge, energy, first)


GROUP = 8


def brought(field_ref, flat_refs, field, flats, in_sems):
    flat_copies = [
        pltpu.make_async_copy(ref, flats.at[i], in_sems.at[i]) for i, ref in enumerate(flat_refs)
    ]
    copies = []
    for g in range(field.shape[0] // GROUP):
        here = pl.ds(g * GROUP, GROUP)
        copies.append(pltpu.make_async_copy(field_ref.at[here], field.at[here], in_sems.at[len(flat_refs) + g]))
    for copy in copies[:1] + flat_copies + copies[1:]:
        copy.start()
    return flat_copies, copies


def partial_kernel(
    field_any, east_any, north_any, out_any, cols_any, rows_any,
    field_ref, flat_ref, out_ref, cols_ref, rows_ref, in_sems, out_sems,
):
    channels, row_count, width = field_ref.shape
    flat_copies, copies = brought(field_any, (east_any, north_any), field_ref, flat_ref, in_sems)
    lane = lax.broadcasted_iota(jnp.int32, (row_count, width), 1)
    row = lax.broadcasted_iota(jnp.int32, (row_count, width), 0)
    sub = lax.broadcasted_iota(jnp.int32, (EXTRA, width), 0)
    bottom = at_bottom()
    polar = jnp.logical_or(bottom, lax.axis_index("lat") == 0)
    lower = lax.axis_index("lat") >= lax.axis_size("lat") // 2
    for copy in flat_copies:
        copy.wait()
    east, north = 0.5 * flat_ref[0], 0.5 * flat_ref[1]
    to_east, to_west = DIFFUSION - east, DIFFUSION + east
    to_south, to_north = DIFFUSION - north, DIFFUSION + north
    mid_east = jnp.where(lane == width - 1, 0.0, to_east)
    mid_west = jnp.where(lane == 0, 0.0, to_west)
    mid_south = jnp.where(row == row_count - 1, 0.0, to_south)
    mid_north = jnp.where(row == 0, 0.0, to_north)
    outer = jnp.where(bottom, to_south[row_count - 1 :, :], to_north[:1, :])
    inner = jnp.where(bottom, to_north[:1, :], to_south[row_count - 1 :, :])
    pick_lane = lax.broadcasted_iota(jnp.int32, (16, width), 1)
    pick_row = lax.broadcasted_iota(jnp.int32, (16, width), 0)
    pick = jnp.where(pick_lane == jnp.where(pick_row == 0, 0, width - 1), 1.0, 0.0)
    pick = jnp.where(pick_row < 2, pick, 0.0).astype(jnp.bfloat16)

    def ends(cells):
        contract = (((1,), (1,)), ((), ()))
        return lax.dot_general(pick, cells.astype(jnp.bfloat16), contract, preferred_element_type=jnp.float32)

    rims = ends(jnp.concatenate([to_west, to_east], axis=0))
    rims = jnp.where(lane[:1] < row_count, rims[:1], rims[1:2])
    def work(with_step):
        sent = []
        for g, copy in enumerate(copies):
            copy.wait()
            edges = ends(field_ref[g * GROUP : (g + 1) * GROUP].reshape(GROUP * row_count, width))
            cols_ref[0, g : g + 1, :] = edges[0:1]
            cols_ref[1, g : g + 1, :] = edges[1:2]
            for i in range(GROUP):
                c = g * GROUP + i
                if with_step:
                    cells = field_ref[c]
                    stepped = (
                        (1.0 - 4.0 * DIFFUSION) * cells
                        + mid_east * pltpu.roll(cells, width - 1, 1)
                        + mid_west * pltpu.roll(cells, 1, 1)
                        + mid_south * pltpu.roll(cells, row_count - 1, 0)
                        + mid_north * pltpu.roll(cells, 1, 0)
                    ).astype(jnp.bfloat16)
                    for t in range(row_count // 16):
                        at = jnp.where(bottom, row_count - 16 - 16 * t, 16 * t)
                        out_ref[c, pl.ds(pl.multiple_of(at, 16), 16), :] = stepped[16 * t : 16 * t + 16]
                pair = slice(width * (i // 2), width * (i // 2 + 1))
                top_row, low_row = field_ref[c, 0:1, :], field_ref[c, row_count - 1 : row_count, :]
                rows_ref[0, c : c + 1, :] = top_row
                rows_ref[1, c : c + 1, :] = low_row
                tail = jnp.where(sub == 0, edges[0:1, pair], 0.0)
                tail = jnp.where(sub == 1, edges[1:2, pair], tail)
                tail = jnp.where(sub == 2, rims, tail)
                tail = jnp.where(sub == 3, jnp.where(bottom, low_row, top_row), tail)
                tail = jnp.where(sub == 4, -outer if c < 2 * LEV else outer, tail)
                tail = jnp.where(sub == 5, jnp.where(lower, low_row, top_row), tail)
                tail = jnp.where(sub == 6, inner, tail)
                out_ref[c, row_count : row_count + EXTRA, :] = tail.astype(jnp.bfloat16)
            here = pl.ds(g * GROUP, GROUP)
            sent.append(pltpu.make_async_copy(out_ref.at[here], out_any.at[here], out_sems.at[g]))
            sent[-1].start()
        for i, (source, target) in enumerate(((cols_ref, cols_any), (rows_ref, rows_any))):
            sent.append(pltpu.make_async_copy(source, target, out_sems.at[len(copies) + i]))
            sent[-1].start()
        for copy in sent:
            copy.wait()

    pl.when(polar)(functools.partial(work, True))
    pl.when(jnp.logical_not(polar))(functools.partial(work, False))


def partial_step(field, east_speed, north_speed):
    channels, row_count, width = field.shape
    anywhere = pl.BlockSpec(memory_space=pl.ANY)
    payload = (channels, row_count + EXTRA, width)
    cols, rows = (2, channels // GROUP, GROUP * row_count), (2, channels, width)
    return pl.pallas_call(
        partial_kernel,
        out_shape=(
            jax.ShapeDtypeStruct(payload, jnp.bfloat16),
            jax.ShapeDtypeStruct(cols, jnp.float32),
            jax.ShapeDtypeStruct(rows, jnp.float32),
        ),
        in_specs=[anywhere] * 3,
        out_specs=(anywhere, anywhere, anywhere),
        scratch_shapes=[
            pltpu.VMEM(field.shape, jnp.float32),
            pltpu.VMEM((2, row_count, width), jnp.float32),
            pltpu.VMEM(payload, jnp.bfloat16),
            pltpu.VMEM(cols, jnp.float32),
            pltpu.VMEM(rows, jnp.float32),
            pltpu.SemaphoreType.DMA((channels // GROUP + 2,)),
            pltpu.SemaphoreType.DMA((channels // GROUP + 2,)),
        ],
        cost_estimate=pl.CostEstimate(flops=field.size * 9, bytes_accessed=field.size * 6, transcendentals=0),
    )(field, east_speed, north_speed)


def merge_kernel(back_ref, full_ref, out_ref, energy_ref, wide_ref, sems):
    del full_ref
    channels, row_count, width = out_ref.shape
    bottom = at_bottom()
    polar = jnp.logical_or(bottom, lax.axis_index("lat") == 0)
    shift = lax.rem(width - CAP * lax.axis_index("lon"), width)
    group = 8

    @pl.when(polar)
    def _():
        copies = []
        for g in range(channels // group):
            for c in range(g * group, (g + 1) * group):
                for t in range(row_count // 16):
                    at = jnp.where(bottom, row_count - 16 - 16 * t, 16 * t)
                    wide_ref[c, 16 * t : 16 * t + 16, :] = back_ref[
                        c, pl.ds(pl.multiple_of(at, 16), 16), :
                    ].astype(jnp.float32)
            here = pl.ds(g * group, group)
            copies.append(pltpu.make_async_copy(wide_ref.at[here], out_ref.at[here], sems.at[g]))
            copies[-1].start()
        total = jnp.zeros((EXTRA, width), jnp.float32)
        for c in range(channels):
            total = total + back_ref[c, row_count : row_count + EXTRA, :].astype(jnp.float32)
        energy = jnp.sum(total, axis=0, keepdims=True) * (1.0 / (channels * channels * width))
        energy = pltpu.roll(jnp.broadcast_to(energy, (8, width)), shift, 1)
        energy_ref[...] = energy[:1, :CAP]
        for copy in copies:
            copy.wait()

    @pl.when(jnp.logical_not(polar))
    def _():
        energy_ref[...] = jnp.zeros((1, CAP), jnp.float32)


def merge(back, full):
    channels, row_count, width = full.shape
    anywhere = pl.BlockSpec(memory_space=pl.ANY)
    return pl.pallas_call(
        merge_kernel,
        out_shape=(
            jax.ShapeDtypeStruct(full.shape, jnp.float32),
            jax.ShapeDtypeStruct((1, CAP), jnp.float32),
        ),
        in_specs=[VMEM, anywhere],
        out_specs=(anywhere, VMEM),
        input_output_aliases={1: 0},
        scratch_shapes=[pltpu.VMEM(full.shape, jnp.float32), pltpu.SemaphoreType.DMA((channels // 8,))],
        compiler_params=pltpu.CompilerParams(vmem_limit_bytes=16 * 1024 * 1024),
    )(back, full)


def step_kernel(
    field_any, east_any, north_any, up_ref, down_ref, west_col_ref, east_col_ref, out_any,
    field_ref, flat_ref, out_ref, col_ref, in_sems, out_sems,
):
    channels, row_count, width = field_ref.shape
    flat_copies, copies = brought(field_any, (east_any, north_any), field_ref, flat_ref, in_sems)
    lane = lax.broadcasted_iota(jnp.int32, (row_count, width), 1)
    row = lax.broadcasted_iota(jnp.int32, (row_count, width), 0)
    for c in range(channels):
        g, at = c // GROUP, row_count * (c % GROUP)
        col_ref[2 * c : 2 * c + 1, :row_count] = east_col_ref[g : g + 1, at : at + row_count]
        col_ref[2 * c + 1 : 2 * c + 2, :row_count] = west_col_ref[g : g + 1, at : at + row_count]
    cols = col_ref[...].T[:row_count, :]
    cols = jnp.concatenate([cols, jnp.zeros((row_count, width - 2 * channels), jnp.float32)], axis=1)
    for copy in flat_copies:
        copy.wait()
    east, north = 0.5 * flat_ref[0], 0.5 * flat_ref[1]
    to_east, to_west = DIFFUSION - east, DIFFUSION + east
    to_south, to_north = DIFFUSION - north, DIFFUSION + north
    sent = []
    for g, copy in enumerate(copies):
        copy.wait()
        for c in range(g * GROUP, (g + 1) * GROUP):
            cells = field_ref[c]
            rim = pltpu.roll(cols, (width - 2 * c - 1) % width, 1)
            west = jnp.where(lane == 0, rim, pltpu.roll(cells, 1, 1))
            east = jnp.where(lane == width - 1, rim, pltpu.roll(cells, width - 1, 1))
            up = jnp.where(row == 0, up_ref[c : c + 1, :], pltpu.roll(cells, 1, 0))
            down = jnp.where(row == row_count - 1, down_ref[c : c + 1, :], pltpu.roll(cells, row_count - 1, 0))
            out_ref[c] = (
                (1.0 - 4.0 * DIFFUSION) * cells + to_east * east + to_west * west + to_south * down + to_north * up
            )
        here = pl.ds(g * GROUP, GROUP)
        sent.append(pltpu.make_async_copy(out_ref.at[here], out_any.at[here], out_sems.at[g]))
        sent[-1].start()
    for copy in sent:
        copy.wait()


def step(field, east_speed, north_speed, up, down, west_col, east_col):
    channels, row_count, width = field.shape
    anywhere = pl.BlockSpec(memory_space=pl.ANY)
    return pl.pallas_call(
        step_kernel,
        out_shape=jax.ShapeDtypeStruct(field.shape, jnp.float32),
        in_specs=[anywhere] * 3 + [VMEM] * 4,
        out_specs=anywhere,
        scratch_shapes=[
            pltpu.VMEM(field.shape, jnp.float32),
            pltpu.VMEM((2, row_count, width), jnp.float32),
            pltpu.VMEM(field.shape, jnp.float32),
            pltpu.VMEM((2 * channels, width), jnp.float32),
            pltpu.SemaphoreType.DMA((channels // GROUP + 2,)),
            pltpu.SemaphoreType.DMA((channels // GROUP,)),
        ],
        cost_estimate=pl.CostEstimate(flops=field.size * 9, bytes_accessed=field.size * 8, transcendentals=0),
    )(field, east_speed, north_speed, up, down, west_col, east_col)


def on_device(lat_count, lon_count, atmosphere, east_speed, north_speed, owners, cutoff):
    channels, row_count, width = atmosphere.shape
    bottom = at_bottom()

    groups = [rank_order(lon_count)]
    exchange = functools.partial(
        lax.all_to_all, axis_name="lon", split_axis=0, concat_axis=0, tiled=True, axis_index_groups=groups
    )
    sent, cols, edge_rows = partial_step(atmosphere, east_speed, north_speed)
    received = exchange(sent)
    owner_row = jnp.where(bottom, owners[1, :, 0], owners[0, :, 0])
    cut_row = jnp.where(bottom, cutoff[1], cutoff[0])
    same = owner_row[:, None] == owner_row[None, :]
    earlier = lax.iota(jnp.int32, row_count)[:, None] > lax.iota(jnp.int32, row_count)[None, :]
    rank = jnp.sum(jnp.logical_and(same, earlier).astype(jnp.int32), axis=1)
    slot = owner_row * CAP + rank

    def placed(values):
        blocks = values.reshape(row_count // 16, 16)
        return jnp.where(bottom, blocks[::-1], blocks).reshape(row_count, 1)

    def next_band(rows):
        pairs = [(b * lon_count + o, (b ^ 1) * lon_count + o) for b in range(lat_count) for o in range(lon_count)]
        return lax.ppermute(rows[:, row_count + 5], ("lat", "lon"), pairs)

    west_col = lax.ppermute(cols[1], "lon", [(o, (o + 1) % lon_count) for o in range(lon_count)])
    east_col = lax.ppermute(cols[0], "lon", [((o + 1) % lon_count, o) for o in range(lon_count)])
    up = lax.ppermute(edge_rows[1], "lat", [(b, b + 1) for b in range(lat_count - 1)])
    down = lax.ppermute(edge_rows[0], "lat", [(b + 1, b) for b in range(lat_count - 1)])
    received, halos = lax.optimization_barrier((received, (up, down, west_col, east_col)))
    filtered = filter_rows(received, next_band, placed(cut_row), placed(slot))
    returned = exchange(filtered)
    full = step(atmosphere, east_speed, north_speed, *halos)
    return merge(returned, full)


def solution(mesh):
    in_specs = (P(None, "lat", "lon"), P("lat", "lon"), P("lat", "lon"), P(), P())
    out_specs = (P(None, "lat", "lon"), P("lat", "lon"))
    return jax.shard_map(
        functools.partial(on_device, mesh.shape["lat"], mesh.shape["lon"]),
        mesh=mesh,
        in_specs=in_specs,
        out_specs=out_specs,
        check_vma=False,
    )
```

```python
import functools
import math

import jax
import jax.numpy as jnp
import ml_dtypes
import numpy as np
from jax import lax
from jax.experimental import pallas as pl
from jax.experimental.pallas import tpu as pltpu
from jax.sharding import PartitionSpec as P

LEV = 8
DIFFUSION = 0.1
CAP = 4
EXTRA = 8
VMEM = pl.BlockSpec(memory_space=pltpu.VMEM)


def real_forward(values):
    n = len(values)
    if n == 1:
        return [(values[0], None)]
    even = real_forward(values[0::2])
    odd = real_forward(values[1::2])
    half = n // 2
    out = [None] * (half + 1)
    for k in range(half // 2 + 1):
        er, ei = even[k]
        orr, oi = odd[k]
        if k == 0:
            out[0] = (er + orr, None)
            out[half] = (er - orr, None)
        elif 2 * k == half:
            out[k] = (er, -orr)
        else:
            c, s = math.cos(2 * math.pi * k / n), math.sin(2 * math.pi * k / n)
            if 8 * k == n:
                tr, ti = (orr + oi) * c, (oi - orr) * c
            else:
                tr, ti = orr * c + oi * s, oi * c - orr * s
            out[k] = (er + tr, ei + ti)
            out[half - k] = (er - tr, ti - ei)
    return out


def real_inverse(coefs):
    half = len(coefs) - 1
    if half == 0:
        return [coefs[0][0]]
    n = 2 * half
    even, odd = [None] * (half // 2 + 1), [None] * (half // 2 + 1)
    for k in range(half // 2 + 1):
        ar, ai = coefs[k]
        br, bi = coefs[half - k]
        if k == 0:
            even[0], odd[0] = (ar + br, None), (ar - br, None)
        elif 2 * k == half:
            even[k], odd[k] = (ar + ar, None), (-(ai + ai), None)
        else:
            even[k] = (ar + br, ai - bi)
            dr, di = ar - br, ai + bi
            c, s = math.cos(2 * math.pi * k / n), math.sin(2 * math.pi * k / n)
            if 8 * k == n:
                odd[k] = ((dr - di) * c, (dr + di) * c)
            else:
                odd[k] = (dr * c - di * s, di * c + dr * s)
    if half == 1:
        return [even[0][0], odd[0][0]]
    first, second = real_inverse(even), real_inverse(odd)
    return [v for pair in zip(first, second) for v in pair]


@functools.lru_cache(None)
def tables(parts, width):
    length = parts * width
    steps = np.arange(width)[:, None] * np.arange(width)[None, :] % width
    angle = 2 * np.pi * steps / width
    cos, sin = np.cos(angle), np.sin(angle)
    forward = np.block([[cos, -sin], [sin, cos]])
    inverse = forward.T / length

    def halves(table):
        high = table.astype(ml_dtypes.bfloat16)
        low = (table - high.astype(np.float64)).astype(ml_dtypes.bfloat16)
        return np.stack([high, low])

    turn = 2 * np.pi * np.arange(parts // 2 + 1)[:, None] * np.arange(width)[None, :] / length
    twiddle = np.stack([np.cos(turn), np.sin(turn)]).astype(np.float32)
    return np.stack([halves(forward), halves(inverse)]), twiddle


def split_halves(value):
    high = value.astype(jnp.bfloat16)
    return high, (value - high.astype(jnp.float32)).astype(jnp.bfloat16)


def add_edges(values, edge, lane):
    width = lane.shape[1]
    rim = jnp.logical_or(lane == 0, lane == width - 1)
    return [
        value + jnp.where(rim, pltpu.roll(edge, (width - 2 * s - 1) % width, 1), 0.0)
        for s, value in enumerate(values)
    ]


def rank_order(parts):
    quarter = parts // 4
    return [q * quarter + quarter - 1 - i for q in (3, 1, 0, 2) for i in range(quarter)]


def at_bottom():
    return lax.axis_index("lat") == lax.axis_size("lat") - 1


def filter_kernel(parts, first_block, block_count, rows_ref, *refs):
    order = rank_order(parts)
    place = [order.index(s) for s in range(parts)]
    last_call = first_block > 0
    if last_call:
        halo_ref, cut_ref, slot_ref, mat_ref, tw_ref, edge_ref, before_ref, earlier_ref, out_ref, *refs = refs
    else:
        cut_ref, slot_ref, mat_ref, tw_ref, done_ref, edge_ref, energy_ref, *refs = refs
    extra_ref, pair_ref, high_ref, low_ref, wave_ref, *refs = refs
    count = parts // 2 + 1
    row_count, width = rows_ref.shape[1] - EXTRA, rows_ref.shape[2]
    bottom = at_bottom()
    rows_here = 16 * block_count
    if last_call:
        done_ref, sems = refs
        copies = [pltpu.make_async_copy(earlier_ref, out_ref.at[:, pl.ds(0, 16 * first_block)], sems.at[0])]
        copies[0].start()

    for i in range(parts):
        extra_ref[order[i] * EXTRA : (order[i] + 1) * EXTRA, :] = rows_ref[i, row_count : row_count + EXTRA, :].astype(jnp.float32)

    def extra(i):
        return extra_ref[pl.ds(i, parts, stride=EXTRA), :]

    if last_call:
        halo = halo_ref[...].astype(jnp.float32)
        for i in range(parts):
            pair_ref[order[i] : order[i] + 1, :] = halo[i : i + 1, :]
        border = extra(6) * pair_ref[:parts, :]
        border_row = jnp.where(bottom, 0, 15)
    else:
        odd = lax.axis_index("lon") % 2 == 0
        first, last = (jnp.where(odd, pltpu.roll(extra(i), width // 2, 1), extra(i)) for i in range(2))
        coef = extra(2)
        from_west = coef * pltpu.roll(last, 1, 0)
        from_east = pltpu.roll(coef, width // 2, 1) * pltpu.roll(first, parts - 1, 0)
        pair_ref[pl.ds(0, parts, stride=2), :] = from_east
        pair_ref[pl.ds(1, parts, stride=2), :] = from_west
        edge = pair_ref[...].T[:row_count, :]
        edge_ref[...] = jnp.concatenate([edge, jnp.zeros((row_count, width - 2 * parts), jnp.float32)], axis=1)
        border = extra(4) * pltpu.roll(extra(3), parts // 2, 0)
        border_row = jnp.where(bottom, 15, 0)
    lane = lax.broadcasted_iota(jnp.int32, (8, width), 1)
    sub = lax.broadcasted_iota(jnp.int32, (8, width), 0)

    for block in range(block_count):
        at = slice(16 * block, 16 * block + 16)
        source = first_block + block
        natural = jnp.where(bottom, 48 - 16 * source, 16 * source)
        has_border = source == (3 if last_call else 0)
        halves = []
        for part in range(2):
            values = [
                rows_ref[place[s], 16 * source : 16 * source + 16, :].astype(jnp.float32)[part * 8 : part * 8 + 8]
                for s in range(parts)
            ]
            values = add_edges(values, edge_ref[pl.ds(pl.multiple_of(natural + 8 * part, 8), 8), :], lane)
            if has_border:
                here = sub + 8 * part == border_row
                values = [
                    v + jnp.where(here, border[s : s + 1, :], 0.0) for s, v in enumerate(values)
                ]
            spun = []
            for k, (re, im) in enumerate(real_forward(values)):
                if k == 0:
                    spun.append((re, jnp.zeros_like(re)))
                    continue
                c, sn = tw_ref[0, k : k + 1, :], tw_ref[1, k : k + 1, :]
                if im is None:
                    spun.append((re * c, -(re * sn)))
                else:
                    spun.append((re * c + im * sn, im * c - re * sn))
            halves.append(spun)
        for k in range(count):
            for side in range(2):
                value = jnp.concatenate([halves[0][k][side], halves[1][k][side]], axis=0)
                high, low = split_halves(value)
                lanes = slice(side * width, (side + 1) * width)
                high_ref[k, at, lanes] = high
                low_ref[k, at, lanes] = low

    cut = cut_ref[16 * first_block : 16 * first_block + rows_here, :]
    wide = lax.broadcasted_iota(jnp.int32, (rows_here, width), 1)
    wide = jnp.concatenate([wide, wide], axis=1)
    dot = functools.partial(jnp.dot, preferred_element_type=jnp.float32)
    step = 4 if block_count > 1 else 9
    for k0 in range(0, count, step):
        k1 = min(count, k0 + step)
        flat = ((k1 - k0) * rows_here, 2 * width)
        high, low = high_ref[k0:k1].reshape(flat), low_ref[k0:k1].reshape(flat)
        coef = dot(high, mat_ref[0, 0]) + dot(low, mat_ref[0, 0]) + dot(high, mat_ref[0, 1])
        kept = []
        for k in range(k0, k1):
            wave = k + parts * wide
            keep = jnp.minimum(wave, parts * width - wave) < cut
            kept.append(jnp.where(keep, coef[(k - k0) * rows_here : (k - k0 + 1) * rows_here], 0.0))
        high, low = split_halves(jnp.concatenate(kept, axis=0))
        wave = dot(high, mat_ref[1, 0]) + dot(low, mat_ref[1, 0]) + dot(high, mat_ref[1, 1])
        wave_ref[k0:k1] = wave.reshape(k1 - k0, rows_here, 2 * width)

    energy = before_ref[...] if last_call else jnp.zeros((8, width), jnp.float32)
    for block in range(block_count):
        source = first_block + block
        halves = []
        for part in range(2):
            here = slice(16 * block + 8 * part, 16 * block + 8 * part + 8)
            coefs = []
            for k in range(count):
                re, im = wave_ref[k, here, :width], wave_ref[k, here, width:]
                if k == 0:
                    coefs.append((re, None))
                    continue
                c, sn = tw_ref[0, k : k + 1, :], tw_ref[1, k : k + 1, :]
                coefs.append((re * c - im * sn, None if 2 * k == parts else im * c + re * sn))
            values = real_inverse(coefs)
            total = values[0] * values[0]
            for value in values[1:]:
                total = total + value * value
            row_sum = jnp.sum(total, axis=1, keepdims=True)
            slots = slot_ref[16 * source + 8 * part : 16 * source + 8 * part + 8, :]
            energy = energy + jnp.where(slots == lane, row_sum, 0.0)
            halves.append(values)
        for s in range(parts):
            done_ref[place[s], 16 * block : 16 * block + 16, :] = jnp.concatenate(
                [halves[0][s], halves[1][s]], axis=0
            ).astype(jnp.bfloat16)
    if last_call:
        total = jnp.sum(energy, axis=0, keepdims=True)
        high = total.astype(jnp.bfloat16).astype(jnp.float32)
        tail = jnp.where(sub == 0, high, jnp.where(sub == 1, total - high, 0.0)).astype(jnp.bfloat16)
        for s in range(parts):
            done_ref[s, rows_here : rows_here + EXTRA, :] = tail
        copies.append(
            pltpu.make_async_copy(done_ref, out_ref.at[:, pl.ds(16 * first_block, rows_here + EXTRA)], sems.at[1])
        )
        copies[-1].start()
        for copy in copies:
            copy.wait()
    else:
        energy_ref[...] = energy


def filter_rows(rows, halo, cut, slot):
    parts, row_count, width = rows.shape
    row_count -= EXTRA
    count = parts // 2 + 1
    mats, twiddle = tables(parts, width)
    operands = (cut, slot, jnp.asarray(mats), jnp.asarray(twiddle))
    anywhere = pl.BlockSpec(memory_space=pl.ANY)

    def call(first_block, block_count, out_shape, out_specs, own, *args):
        rows_here = 16 * block_count
        return pl.pallas_call(
            functools.partial(filter_kernel, parts, first_block, block_count),
            out_shape=out_shape,
            in_specs=[VMEM] * len(args),
            out_specs=out_specs,
            scratch_shapes=[
                pltpu.VMEM((parts * EXTRA, width), jnp.float32),
                pltpu.VMEM((2 * parts, width), jnp.float32),
                pltpu.VMEM((count, rows_here, 2 * width), jnp.bfloat16),
                pltpu.VMEM((count, rows_here, 2 * width), jnp.bfloat16),
                pltpu.VMEM((count, rows_here, 2 * width), jnp.float32),
                *own,
            ],
            compiler_params=pltpu.CompilerParams(vmem_limit_bytes=24 * 1024 * 1024),
            cost_estimate=pl.CostEstimate(
                flops=rows_here * parts * width * 8000, bytes_accessed=rows.size * 4, transcendentals=0
            ),
        )(*args)

    earlier = jax.ShapeDtypeStruct((parts, row_count - 16, width), jnp.bfloat16)
    whole = jax.ShapeDtypeStruct(rows.shape, jnp.bfloat16)
    edge = jax.ShapeDtypeStruct((row_count, width), jnp.float32)
    energy = jax.ShapeDtypeStruct((8, width), jnp.float32)
    halo_rows = halo(rows)
    first, edge, energy = call(0, 3, (earlier, edge, energy), (VMEM, VMEM, VMEM), [], rows, *operands)
    own = [pltpu.VMEM((parts, 16 + EXTRA, width), jnp.bfloat16), pltpu.SemaphoreType.DMA((2,))]
    return call(3, 1, whole, anywhere, own, rows, halo_rows, *operands, edge, energy, first)


GROUP = 8


def brought(field_ref, flat_refs, field, flats, in_sems):
    flat_copies = [
        pltpu.make_async_copy(ref, flats.at[i], in_sems.at[i]) for i, ref in enumerate(flat_refs)
    ]
    copies = []
    for g in range(field.shape[0] // GROUP):
        here = pl.ds(g * GROUP, GROUP)
        copies.append(pltpu.make_async_copy(field_ref.at[here], field.at[here], in_sems.at[len(flat_refs) + g]))
    for copy in copies[:1] + flat_copies + copies[1:]:
        copy.start()
    return flat_copies, copies


def partial_kernel(
    field_any, east_any, north_any, out_any, cols_any, rows_any,
    field_ref, flat_ref, out_ref, cols_ref, rows_ref, in_sems, out_sems,
):
    channels, row_count, width = field_ref.shape
    flat_copies, copies = brought(field_any, (east_any, north_any), field_ref, flat_ref, in_sems)
    lane = lax.broadcasted_iota(jnp.int32, (row_count, width), 1)
    row = lax.broadcasted_iota(jnp.int32, (row_count, width), 0)
    sub = lax.broadcasted_iota(jnp.int32, (EXTRA, width), 0)
    bottom = at_bottom()
    polar = jnp.logical_or(bottom, lax.axis_index("lat") == 0)
    lower = lax.axis_index("lat") >= lax.axis_size("lat") // 2
    for copy in flat_copies:
        copy.wait()
    east, north = 0.5 * flat_ref[0], 0.5 * flat_ref[1]
    to_east, to_west = DIFFUSION - east, DIFFUSION + east
    to_south, to_north = DIFFUSION - north, DIFFUSION + north
    mid_east = jnp.where(lane == width - 1, 0.0, to_east)
    mid_west = jnp.where(lane == 0, 0.0, to_west)
    mid_south = jnp.where(row == row_count - 1, 0.0, to_south)
    mid_north = jnp.where(row == 0, 0.0, to_north)
    outer = jnp.where(bottom, to_south[row_count - 1 :, :], to_north[:1, :])
    inner = jnp.where(bottom, to_north[:1, :], to_south[row_count - 1 :, :])
    pick_lane = lax.broadcasted_iota(jnp.int32, (16, width), 1)
    pick_row = lax.broadcasted_iota(jnp.int32, (16, width), 0)
    pick = jnp.where(pick_lane == jnp.where(pick_row == 0, 0, width - 1), 1.0, 0.0)
    pick = jnp.where(pick_row < 2, pick, 0.0).astype(jnp.bfloat16)

    def ends(cells):
        contract = (((1,), (1,)), ((), ()))
        return lax.dot_general(pick, cells.astype(jnp.bfloat16), contract, preferred_element_type=jnp.float32)

    rims = ends(jnp.concatenate([to_west, to_east], axis=0))
    rims = jnp.where(lane[:1] < row_count, rims[:1], rims[1:2])
    def work(with_step):
        sent = []
        for g, copy in enumerate(copies):
            copy.wait()
            edges = ends(field_ref[g * GROUP : (g + 1) * GROUP].reshape(GROUP * row_count, width))
            cols_ref[0, g : g + 1, :] = edges[0:1]
            cols_ref[1, g : g + 1, :] = edges[1:2]
            for i in range(GROUP):
                c = g * GROUP + i
                if with_step:
                    cells = field_ref[c]
                    stepped = (
                        (1.0 - 4.0 * DIFFUSION) * cells
                        + mid_east * pltpu.roll(cells, width - 1, 1)
                        + mid_west * pltpu.roll(cells, 1, 1)
                        + mid_south * pltpu.roll(cells, row_count - 1, 0)
                        + mid_north * pltpu.roll(cells, 1, 0)
                    ).astype(jnp.bfloat16)
                    for t in range(row_count // 16):
                        at = jnp.where(bottom, row_count - 16 - 16 * t, 16 * t)
                        out_ref[c, pl.ds(pl.multiple_of(at, 16), 16), :] = stepped[16 * t : 16 * t + 16]
                pair = slice(width * (i // 2), width * (i // 2 + 1))
                top_row, low_row = field_ref[c, 0:1, :], field_ref[c, row_count - 1 : row_count, :]
                rows_ref[0, c : c + 1, :] = top_row
                rows_ref[1, c : c + 1, :] = low_row
                tail = jnp.where(sub == 0, edges[0:1, pair], 0.0)
                tail = jnp.where(sub == 1, edges[1:2, pair], tail)
                tail = jnp.where(sub == 2, rims, tail)
                tail = jnp.where(sub == 3, jnp.where(bottom, low_row, top_row), tail)
                tail = jnp.where(sub == 4, -outer if c < 2 * LEV else outer, tail)
                tail = jnp.where(sub == 5, jnp.where(lower, low_row, top_row), tail)
                tail = jnp.where(sub == 6, inner, tail)
                out_ref[c, row_count : row_count + EXTRA, :] = tail.astype(jnp.bfloat16)
            here = pl.ds(g * GROUP, GROUP)
            sent.append(pltpu.make_async_copy(out_ref.at[here], out_any.at[here], out_sems.at[g]))
            sent[-1].start()
        for i, (source, target) in enumerate(((cols_ref, cols_any), (rows_ref, rows_any))):
            sent.append(pltpu.make_async_copy(source, target, out_sems.at[len(copies) + i]))
            sent[-1].start()
        for copy in sent:
            copy.wait()

    pl.when(polar)(functools.partial(work, True))
    pl.when(jnp.logical_not(polar))(functools.partial(work, False))


def partial_step(field, east_speed, north_speed):
    channels, row_count, width = field.shape
    anywhere = pl.BlockSpec(memory_space=pl.ANY)
    payload = (channels, row_count + EXTRA, width)
    cols, rows = (2, channels // GROUP, GROUP * row_count), (2, channels, width)
    return pl.pallas_call(
        partial_kernel,
        out_shape=(
            jax.ShapeDtypeStruct(payload, jnp.bfloat16),
            jax.ShapeDtypeStruct(cols, jnp.float32),
            jax.ShapeDtypeStruct(rows, jnp.float32),
        ),
        in_specs=[anywhere] * 3,
        out_specs=(anywhere, anywhere, anywhere),
        scratch_shapes=[
            pltpu.VMEM(field.shape, jnp.float32),
            pltpu.VMEM((2, row_count, width), jnp.float32),
            pltpu.VMEM(payload, jnp.bfloat16),
            pltpu.VMEM(cols, jnp.float32),
            pltpu.VMEM(rows, jnp.float32),
            pltpu.SemaphoreType.DMA((channels // GROUP + 2,)),
            pltpu.SemaphoreType.DMA((channels // GROUP + 2,)),
        ],
        cost_estimate=pl.CostEstimate(flops=field.size * 9, bytes_accessed=field.size * 6, transcendentals=0),
    )(field, east_speed, north_speed)


def merge_kernel(back_ref, full_ref, out_ref, energy_ref, wide_ref, sems):
    del full_ref
    channels, row_count, width = out_ref.shape
    bottom = at_bottom()
    polar = jnp.logical_or(bottom, lax.axis_index("lat") == 0)
    shift = lax.rem(width - CAP * lax.axis_index("lon"), width)
    group = 8

    @pl.when(polar)
    def _():
        copies = []
        for g in range(channels // group):
            for c in range(g * group, (g + 1) * group):
                for t in range(row_count // 16):
                    at = jnp.where(bottom, row_count - 16 - 16 * t, 16 * t)
                    wide_ref[c, 16 * t : 16 * t + 16, :] = back_ref[
                        c, pl.ds(pl.multiple_of(at, 16), 16), :
                    ].astype(jnp.float32)
            here = pl.ds(g * group, group)
            copies.append(pltpu.make_async_copy(wide_ref.at[here], out_ref.at[here], sems.at[g]))
            copies[-1].start()
        total = jnp.zeros((EXTRA, width), jnp.float32)
        for c in range(channels):
            total = total + back_ref[c, row_count : row_count + EXTRA, :].astype(jnp.float32)
        energy = jnp.sum(total, axis=0, keepdims=True) * (1.0 / (channels * channels * width))
        energy = pltpu.roll(jnp.broadcast_to(energy, (8, width)), shift, 1)
        energy_ref[...] = energy[:1, :CAP]
        for copy in copies:
            copy.wait()

    @pl.when(jnp.logical_not(polar))
    def _():
        energy_ref[...] = jnp.zeros((1, CAP), jnp.float32)


def merge(back, full):
    channels, row_count, width = full.shape
    anywhere = pl.BlockSpec(memory_space=pl.ANY)
    return pl.pallas_call(
        merge_kernel,
        out_shape=(
            jax.ShapeDtypeStruct(full.shape, jnp.float32),
            jax.ShapeDtypeStruct((1, CAP), jnp.float32),
        ),
        in_specs=[VMEM, anywhere],
        out_specs=(anywhere, VMEM),
        input_output_aliases={1: 0},
        scratch_shapes=[pltpu.VMEM(full.shape, jnp.float32), pltpu.SemaphoreType.DMA((channels // 8,))],
        compiler_params=pltpu.CompilerParams(vmem_limit_bytes=16 * 1024 * 1024),
    )(back, full)


def step_kernel(
    field_any, east_any, north_any, up_ref, down_ref, west_col_ref, east_col_ref, out_any,
    field_ref, flat_ref, out_ref, col_ref, in_sems, out_sems,
):
    channels, row_count, width = field_ref.shape
    flat_copies, copies = brought(field_any, (east_any, north_any), field_ref, flat_ref, in_sems)
    lane = lax.broadcasted_iota(jnp.int32, (row_count, width), 1)
    row = lax.broadcasted_iota(jnp.int32, (row_count, width), 0)
    for c in range(channels):
        g, at = c // GROUP, row_count * (c % GROUP)
        col_ref[2 * c : 2 * c + 1, :row_count] = east_col_ref[g : g + 1, at : at + row_count]
        col_ref[2 * c + 1 : 2 * c + 2, :row_count] = west_col_ref[g : g + 1, at : at + row_count]
    cols = col_ref[...].T[:row_count, :]
    cols = jnp.concatenate([cols, jnp.zeros((row_count, width - 2 * channels), jnp.float32)], axis=1)
    for copy in flat_copies:
        copy.wait()
    east, north = 0.5 * flat_ref[0], 0.5 * flat_ref[1]
    to_east, to_west = DIFFUSION - east, DIFFUSION + east
    to_south, to_north = DIFFUSION - north, DIFFUSION + north
    sent = []
    for g, copy in enumerate(copies):
        copy.wait()
        for c in range(g * GROUP, (g + 1) * GROUP):
            cells = field_ref[c]
            rim = pltpu.roll(cols, (width - 2 * c - 1) % width, 1)
            west = jnp.where(lane == 0, rim, pltpu.roll(cells, 1, 1))
            east = jnp.where(lane == width - 1, rim, pltpu.roll(cells, width - 1, 1))
            up = jnp.where(row == 0, up_ref[c : c + 1, :], pltpu.roll(cells, 1, 0))
            down = jnp.where(row == row_count - 1, down_ref[c : c + 1, :], pltpu.roll(cells, row_count - 1, 0))
            out_ref[c] = (
                (1.0 - 4.0 * DIFFUSION) * cells + to_east * east + to_west * west + to_south * down + to_north * up
            )
        here = pl.ds(g * GROUP, GROUP)
        sent.append(pltpu.make_async_copy(out_ref.at[here], out_any.at[here], out_sems.at[g]))
        sent[-1].start()
    for copy in sent:
        copy.wait()


def step(field, east_speed, north_speed, up, down, west_col, east_col):
    channels, row_count, width = field.shape
    anywhere = pl.BlockSpec(memory_space=pl.ANY)
    return pl.pallas_call(
        step_kernel,
        out_shape=jax.ShapeDtypeStruct(field.shape, jnp.float32),
        in_specs=[anywhere] * 3 + [VMEM] * 4,
        out_specs=anywhere,
        scratch_shapes=[
            pltpu.VMEM(field.shape, jnp.float32),
            pltpu.VMEM((2, row_count, width), jnp.float32),
            pltpu.VMEM(field.shape, jnp.float32),
            pltpu.VMEM((2 * channels, width), jnp.float32),
            pltpu.SemaphoreType.DMA((channels // GROUP + 2,)),
            pltpu.SemaphoreType.DMA((channels // GROUP,)),
        ],
        cost_estimate=pl.CostEstimate(flops=field.size * 9, bytes_accessed=field.size * 8, transcendentals=0),
    )(field, east_speed, north_speed, up, down, west_col, east_col)


def on_device(lat_count, lon_count, atmosphere, east_speed, north_speed, owners, cutoff):
    channels, row_count, width = atmosphere.shape
    bottom = at_bottom()

    groups = [rank_order(lon_count)]
    exchange = functools.partial(
        lax.all_to_all, axis_name="lon", split_axis=0, concat_axis=0, tiled=True, axis_index_groups=groups
    )
    sent, cols, edge_rows = partial_step(atmosphere, east_speed, north_speed)
    received = exchange(sent)
    owner_row = jnp.where(bottom, owners[1, :, 0], owners[0, :, 0])
    cut_row = jnp.where(bottom, cutoff[1], cutoff[0])
    same = owner_row[:, None] == owner_row[None, :]
    earlier = lax.iota(jnp.int32, row_count)[:, None] > lax.iota(jnp.int32, row_count)[None, :]
    rank = jnp.sum(jnp.logical_and(same, earlier).astype(jnp.int32), axis=1)
    slot = owner_row * CAP + rank

    def placed(values):
        blocks = values.reshape(row_count // 16, 16)
        return jnp.where(bottom, blocks[::-1], blocks).reshape(row_count, 1)

    def next_band(rows):
        pairs = [(b * lon_count + o, (b ^ 1) * lon_count + o) for b in range(lat_count) for o in range(lon_count)]
        return lax.ppermute(rows[:, row_count + 5], ("lat", "lon"), pairs)

    west_col = lax.ppermute(cols[1], "lon", [(o, (o + 1) % lon_count) for o in range(lon_count)])
    east_col = lax.ppermute(cols[0], "lon", [((o + 1) % lon_count, o) for o in range(lon_count)])
    up = lax.ppermute(edge_rows[1], "lat", [(b, b + 1) for b in range(lat_count - 1)])
    down = lax.ppermute(edge_rows[0], "lat", [(b + 1, b) for b in range(lat_count - 1)])
    received, halos = lax.optimization_barrier((received, (up, down, west_col, east_col)))
    filtered = filter_rows(received, next_band, placed(cut_row), placed(slot))
    returned = exchange(filtered)
    full = step(atmosphere, east_speed, north_speed, *halos)
    return merge(returned, full)


def solution(mesh):
    in_specs = (P(None, "lat", "lon"), P("lat", "lon"), P("lat", "lon"), P(), P())
    out_specs = (P(None, "lat", "lon"), P("lat", "lon"))
    return jax.shard_map(
        functools.partial(on_device, mesh.shape["lat"], mesh.shape["lon"]),
        mesh=mesh,
        in_specs=in_specs,
        out_specs=out_specs,
        check_vma=False,
    )
```

```python
import functools
import math

import jax
import jax.numpy as jnp
import ml_dtypes
import numpy as np
from jax import lax
from jax.experimental import pallas as pl
from jax.experimental.pallas import tpu as pltpu
from jax.sharding import PartitionSpec as P

LEV = 8
DIFFUSION = 0.1
CAP = 4
EXTRA = 8
VMEM = pl.BlockSpec(memory_space=pltpu.VMEM)


def real_forward(values):
    n = len(values)
    if n == 1:
        return [(values[0], None)]
    even = real_forward(values[0::2])
    odd = real_forward(values[1::2])
    half = n // 2
    out = [None] * (half + 1)
    for k in range(half // 2 + 1):
        er, ei = even[k]
        orr, oi = odd[k]
        if k == 0:
            out[0] = (er + orr, None)
            out[half] = (er - orr, None)
        elif 2 * k == half:
            out[k] = (er, -orr)
        else:
            c, s = math.cos(2 * math.pi * k / n), math.sin(2 * math.pi * k / n)
            if 8 * k == n:
                tr, ti = (orr + oi) * c, (oi - orr) * c
            else:
                tr, ti = orr * c + oi * s, oi * c - orr * s
            out[k] = (er + tr, ei + ti)
            out[half - k] = (er - tr, ti - ei)
    return out


def real_inverse(coefs):
    half = len(coefs) - 1
    if half == 0:
        return [coefs[0][0]]
    n = 2 * half
    even, odd = [None] * (half // 2 + 1), [None] * (half // 2 + 1)
    for k in range(half // 2 + 1):
        ar, ai = coefs[k]
        br, bi = coefs[half - k]
        if k == 0:
            even[0], odd[0] = (ar + br, None), (ar - br, None)
        elif 2 * k == half:
            even[k], odd[k] = (ar + ar, None), (-(ai + ai), None)
        else:
            even[k] = (ar + br, ai - bi)
            dr, di = ar - br, ai + bi
            c, s = math.cos(2 * math.pi * k / n), math.sin(2 * math.pi * k / n)
            if 8 * k == n:
                odd[k] = ((dr - di) * c, (dr + di) * c)
            else:
                odd[k] = (dr * c - di * s, di * c + dr * s)
    if half == 1:
        return [even[0][0], odd[0][0]]
    first, second = real_inverse(even), real_inverse(odd)
    return [v for pair in zip(first, second) for v in pair]


@functools.lru_cache(None)
def tables(parts, width):
    length = parts * width
    steps = np.arange(width)[:, None] * np.arange(width)[None, :] % width
    angle = 2 * np.pi * steps / width
    cos, sin = np.cos(angle), np.sin(angle)
    forward = np.block([[cos, -sin], [sin, cos]])
    inverse = forward.T / length

    def halves(table):
        high = table.astype(ml_dtypes.bfloat16)
        low = (table - high.astype(np.float64)).astype(ml_dtypes.bfloat16)
        return np.stack([high, low])

    turn = 2 * np.pi * np.arange(parts // 2 + 1)[:, None] * np.arange(width)[None, :] / length
    twiddle = np.stack([np.cos(turn), np.sin(turn)]).astype(np.float32)
    return np.stack([halves(forward), halves(inverse)]), twiddle


def split_halves(value):
    high = value.astype(jnp.bfloat16)
    return high, (value - high.astype(jnp.float32)).astype(jnp.bfloat16)


def add_edges(values, edge, lane):
    width = lane.shape[1]
    rim = jnp.logical_or(lane == 0, lane == width - 1)
    return [
        value + jnp.where(rim, pltpu.roll(edge, (width - 2 * s - 1) % width, 1), 0.0)
        for s, value in enumerate(values)
    ]


def rank_order(parts):
    quarter = parts // 4
    return [q * quarter + quarter - 1 - i for q in (3, 1, 0, 2) for i in range(quarter)]


def at_bottom():
    return lax.axis_index("lat") == lax.axis_size("lat") - 1


def filter_kernel(parts, first_block, block_count, rows_ref, *refs):
    order = rank_order(parts)
    place = [order.index(s) for s in range(parts)]
    last_call = first_block > 0
    if last_call:
        halo_ref, cut_ref, slot_ref, mat_ref, tw_ref, edge_ref, before_ref, earlier_ref, out_ref, *refs = refs
    else:
        cut_ref, slot_ref, mat_ref, tw_ref, done_ref, edge_ref, energy_ref, *refs = refs
    extra_ref, pair_ref, high_ref, low_ref, wave_ref, *refs = refs
    count = parts // 2 + 1
    row_count, width = rows_ref.shape[1] - EXTRA, rows_ref.shape[2]
    bottom = at_bottom()
    rows_here = 16 * block_count
    if last_call:
        done_ref, sems = refs
        copies = [pltpu.make_async_copy(earlier_ref, out_ref.at[:, pl.ds(0, 16 * first_block)], sems.at[0])]
        copies[0].start()

    for i in range(parts):
        extra_ref[order[i] * EXTRA : (order[i] + 1) * EXTRA, :] = rows_ref[i, row_count : row_count + EXTRA, :].astype(jnp.float32)

    def extra(i):
        return extra_ref[pl.ds(i, parts, stride=EXTRA), :]

    if last_call:
        halo = halo_ref[...].astype(jnp.float32)
        for i in range(parts):
            pair_ref[order[i] : order[i] + 1, :] = halo[i : i + 1, :]
        border = extra(6) * pair_ref[:parts, :]
        border_row = jnp.where(bottom, 0, 15)
    else:
        odd = lax.axis_index("lon") % 2 == 0
        first, last = (jnp.where(odd, pltpu.roll(extra(i), width // 2, 1), extra(i)) for i in range(2))
        coef = extra(2)
        from_west = coef * pltpu.roll(last, 1, 0)
        from_east = pltpu.roll(coef, width // 2, 1) * pltpu.roll(first, parts - 1, 0)
        pair_ref[pl.ds(0, parts, stride=2), :] = from_east
        pair_ref[pl.ds(1, parts, stride=2), :] = from_west
        edge = pair_ref[...].T[:row_count, :]
        edge_ref[...] = jnp.concatenate([edge, jnp.zeros((row_count, width - 2 * parts), jnp.float32)], axis=1)
        border = extra(4) * pltpu.roll(extra(3), parts // 2, 0)
        border_row = jnp.where(bottom, 15, 0)
    lane = lax.broadcasted_iota(jnp.int32, (8, width), 1)
    sub = lax.broadcasted_iota(jnp.int32, (8, width), 0)

    for block in range(block_count):
        at = slice(16 * block, 16 * block + 16)
        source = first_block + block
        natural = jnp.where(bottom, 48 - 16 * source, 16 * source)
        has_border = source == (3 if last_call else 0)
        halves = []
        for part in range(2):
            values = [
                rows_ref[place[s], 16 * source : 16 * source + 16, :].astype(jnp.float32)[part * 8 : part * 8 + 8]
                for s in range(parts)
            ]
            values = add_edges(values, edge_ref[pl.ds(pl.multiple_of(natural + 8 * part, 8), 8), :], lane)
            if has_border:
                here = sub + 8 * part == border_row
                values = [
                    v + jnp.where(here, border[s : s + 1, :], 0.0) for s, v in enumerate(values)
                ]
            spun = []
            for k, (re, im) in enumerate(real_forward(values)):
                if k == 0:
                    spun.append((re, jnp.zeros_like(re)))
                    continue
                c, sn = tw_ref[0, k : k + 1, :], tw_ref[1, k : k + 1, :]
                if im is None:
                    spun.append((re * c, -(re * sn)))
                else:
                    spun.append((re * c + im * sn, im * c - re * sn))
            halves.append(spun)
        for k in range(count):
            for side in range(2):
                value = jnp.concatenate([halves[0][k][side], halves[1][k][side]], axis=0)
                high, low = split_halves(value)
                lanes = slice(side * width, (side + 1) * width)
                high_ref[k, at, lanes] = high
                low_ref[k, at, lanes] = low

    cut = cut_ref[16 * first_block : 16 * first_block + rows_here, :]
    wide = lax.broadcasted_iota(jnp.int32, (rows_here, width), 1)
    wide = jnp.concatenate([wide, wide], axis=1)
    dot = functools.partial(jnp.dot, preferred_element_type=jnp.float32)
    step = 4 if block_count > 1 else 9
    for k0 in range(0, count, step):
        k1 = min(count, k0 + step)
        flat = ((k1 - k0) * rows_here, 2 * width)
        high, low = high_ref[k0:k1].reshape(flat), low_ref[k0:k1].reshape(flat)
        coef = dot(high, mat_ref[0, 0]) + dot(low, mat_ref[0, 0]) + dot(high, mat_ref[0, 1])
        kept = []
        for k in range(k0, k1):
            wave = k + parts * wide
            keep = jnp.minimum(wave, parts * width - wave) < cut
            kept.append(jnp.where(keep, coef[(k - k0) * rows_here : (k - k0 + 1) * rows_here], 0.0))
        high, low = split_halves(jnp.concatenate(kept, axis=0))
        wave = dot(high, mat_ref[1, 0]) + dot(low, mat_ref[1, 0]) + dot(high, mat_ref[1, 1])
        wave_ref[k0:k1] = wave.reshape(k1 - k0, rows_here, 2 * width)

    energy = before_ref[...] if last_call else jnp.zeros((8, width), jnp.float32)
    for block in range(block_count):
        source = first_block + block
        halves = []
        for part in range(2):
            here = slice(16 * block + 8 * part, 16 * block + 8 * part + 8)
            coefs = []
            for k in range(count):
                re, im = wave_ref[k, here, :width], wave_ref[k, here, width:]
                if k == 0:
                    coefs.append((re, None))
                    continue
                c, sn = tw_ref[0, k : k + 1, :], tw_ref[1, k : k + 1, :]
                coefs.append((re * c - im * sn, None if 2 * k == parts else im * c + re * sn))
            values = real_inverse(coefs)
            total = values[0] * values[0]
            for value in values[1:]:
                total = total + value * value
            row_sum = jnp.sum(total, axis=1, keepdims=True)
            slots = slot_ref[16 * source + 8 * part : 16 * source + 8 * part + 8, :]
            energy = energy + jnp.where(slots == lane, row_sum, 0.0)
            halves.append(values)
        for s in range(parts):
            done_ref[place[s], 16 * block : 16 * block + 16, :] = jnp.concatenate(
                [halves[0][s], halves[1][s]], axis=0
            ).astype(jnp.bfloat16)
    if last_call:
        total = jnp.sum(energy, axis=0, keepdims=True)
        high = total.astype(jnp.bfloat16).astype(jnp.float32)
        tail = jnp.where(sub == 0, high, jnp.where(sub == 1, total - high, 0.0)).astype(jnp.bfloat16)
        for s in range(parts):
            done_ref[s, rows_here : rows_here + EXTRA, :] = tail
        copies.append(
            pltpu.make_async_copy(done_ref, out_ref.at[:, pl.ds(16 * first_block, rows_here + EXTRA)], sems.at[1])
        )
        copies[-1].start()
        for copy in copies:
            copy.wait()
    else:
        energy_ref[...] = energy


def filter_rows(rows, halo, cut, slot):
    parts, row_count, width = rows.shape
    row_count -= EXTRA
    count = parts // 2 + 1
    mats, twiddle = tables(parts, width)
    operands = (cut, slot, jnp.asarray(mats), jnp.asarray(twiddle))
    anywhere = pl.BlockSpec(memory_space=pl.ANY)

    def call(first_block, block_count, out_shape, out_specs, own, *args):
        rows_here = 16 * block_count
        return pl.pallas_call(
            functools.partial(filter_kernel, parts, first_block, block_count),
            out_shape=out_shape,
            in_specs=[VMEM] * len(args),
            out_specs=out_specs,
            scratch_shapes=[
                pltpu.VMEM((parts * EXTRA, width), jnp.float32),
                pltpu.VMEM((2 * parts, width), jnp.float32),
                pltpu.VMEM((count, rows_here, 2 * width), jnp.bfloat16),
                pltpu.VMEM((count, rows_here, 2 * width), jnp.bfloat16),
                pltpu.VMEM((count, rows_here, 2 * width), jnp.float32),
                *own,
            ],
            compiler_params=pltpu.CompilerParams(vmem_limit_bytes=24 * 1024 * 1024),
            cost_estimate=pl.CostEstimate(
                flops=rows_here * parts * width * 8000, bytes_accessed=rows.size * 4, transcendentals=0
            ),
        )(*args)

    earlier = jax.ShapeDtypeStruct((parts, row_count - 16, width), jnp.bfloat16)
    whole = jax.ShapeDtypeStruct(rows.shape, jnp.bfloat16)
    edge = jax.ShapeDtypeStruct((row_count, width), jnp.float32)
    energy = jax.ShapeDtypeStruct((8, width), jnp.float32)
    halo_rows = halo(rows)
    first, edge, energy = call(0, 3, (earlier, edge, energy), (VMEM, VMEM, VMEM), [], rows, *operands)
    own = [pltpu.VMEM((parts, 16 + EXTRA, width), jnp.bfloat16), pltpu.SemaphoreType.DMA((2,))]
    return call(3, 1, whole, anywhere, own, rows, halo_rows, *operands, edge, energy, first)


GROUP = 16


def brought(field_ref, flat_refs, field, flats, in_sems):
    flat_copies = [
        pltpu.make_async_copy(ref, flats.at[i], in_sems.at[i]) for i, ref in enumerate(flat_refs)
    ]
    copies = []
    for g in range(field.shape[0] // GROUP):
        here = pl.ds(g * GROUP, GROUP)
        copies.append(pltpu.make_async_copy(field_ref.at[here], field.at[here], in_sems.at[len(flat_refs) + g]))
    for copy in flat_copies + copies:
        copy.start()
    return flat_copies, copies


def partial_kernel(
    field_any, east_any, north_any, out_any, cols_any, rows_any,
    field_ref, flat_ref, out_ref, cols_ref, rows_ref, in_sems, out_sems,
):
    channels, row_count, width = field_ref.shape
    flat_copies, copies = brought(field_any, (east_any, north_any), field_ref, flat_ref, in_sems)
    lane = lax.broadcasted_iota(jnp.int32, (row_count, width), 1)
    row = lax.broadcasted_iota(jnp.int32, (row_count, width), 0)
    sub = lax.broadcasted_iota(jnp.int32, (EXTRA, width), 0)
    bottom = at_bottom()
    polar = jnp.logical_or(bottom, lax.axis_index("lat") == 0)
    lower = lax.axis_index("lat") >= lax.axis_size("lat") // 2
    for copy in flat_copies:
        copy.wait()
    east, north = 0.5 * flat_ref[0], 0.5 * flat_ref[1]
    to_east, to_west = DIFFUSION - east, DIFFUSION + east
    to_south, to_north = DIFFUSION - north, DIFFUSION + north
    mid_east = jnp.where(lane == width - 1, 0.0, to_east)
    mid_west = jnp.where(lane == 0, 0.0, to_west)
    mid_south = jnp.where(row == row_count - 1, 0.0, to_south)
    mid_north = jnp.where(row == 0, 0.0, to_north)
    outer = jnp.where(bottom, to_south[row_count - 1 :, :], to_north[:1, :])
    inner = jnp.where(bottom, to_north[:1, :], to_south[row_count - 1 :, :])
    pick_lane = lax.broadcasted_iota(jnp.int32, (16, width), 1)
    pick_row = lax.broadcasted_iota(jnp.int32, (16, width), 0)
    pick = jnp.where(pick_lane == jnp.where(pick_row == 0, 0, width - 1), 1.0, 0.0)
    pick = jnp.where(pick_row < 2, pick, 0.0).astype(jnp.bfloat16)

    def ends(cells):
        contract = (((1,), (1,)), ((), ()))
        return lax.dot_general(pick, cells.astype(jnp.bfloat16), contract, preferred_element_type=jnp.float32)

    rims = ends(jnp.concatenate([to_west, to_east], axis=0))
    rims = jnp.where(lane[:1] < row_count, rims[:1], rims[1:2])
    def work(with_step):
        sent = []
        for g, copy in enumerate(copies):
            copy.wait()
            edges = ends(field_ref[g * GROUP : (g + 1) * GROUP].reshape(GROUP * row_count, width))
            cols_ref[0, g : g + 1, :] = edges[0:1]
            cols_ref[1, g : g + 1, :] = edges[1:2]
            for i in range(GROUP):
                c = g * GROUP + i
                if with_step:
                    cells = field_ref[c]
                    stepped = (
                        (1.0 - 4.0 * DIFFUSION) * cells
                        + mid_east * pltpu.roll(cells, width - 1, 1)
                        + mid_west * pltpu.roll(cells, 1, 1)
                        + mid_south * pltpu.roll(cells, row_count - 1, 0)
                        + mid_north * pltpu.roll(cells, 1, 0)
                    ).astype(jnp.bfloat16)
                    for t in range(row_count // 16):
                        at = jnp.where(bottom, row_count - 16 - 16 * t, 16 * t)
                        out_ref[c, pl.ds(pl.multiple_of(at, 16), 16), :] = stepped[16 * t : 16 * t + 16]
                pair = slice(width * (i // 2), width * (i // 2 + 1))
                top_row, low_row = field_ref[c, 0:1, :], field_ref[c, row_count - 1 : row_count, :]
                rows_ref[0, c : c + 1, :] = top_row
                rows_ref[1, c : c + 1, :] = low_row
                tail = jnp.where(sub == 0, edges[0:1, pair], 0.0)
                tail = jnp.where(sub == 1, edges[1:2, pair], tail)
                tail = jnp.where(sub == 2, rims, tail)
                tail = jnp.where(sub == 3, jnp.where(bottom, low_row, top_row), tail)
                tail = jnp.where(sub == 4, -outer if c < 2 * LEV else outer, tail)
                tail = jnp.where(sub == 5, jnp.where(lower, low_row, top_row), tail)
                tail = jnp.where(sub == 6, inner, tail)
                out_ref[c, row_count : row_count + EXTRA, :] = tail.astype(jnp.bfloat16)
            here = pl.ds(g * GROUP, GROUP)
            rows = pl.ds(0, row_count + EXTRA) if with_step else pl.ds(row_count, EXTRA)
            sent.append(pltpu.make_async_copy(out_ref.at[here, rows], out_any.at[here, rows], out_sems.at[g]))
            sent[-1].start()
        for i, (source, target) in enumerate(((cols_ref, cols_any), (rows_ref, rows_any))):
            sent.append(pltpu.make_async_copy(source, target, out_sems.at[len(copies) + i]))
            sent[-1].start()
        for copy in sent:
            copy.wait()

    pl.when(polar)(functools.partial(work, True))
    pl.when(jnp.logical_not(polar))(functools.partial(work, False))


def partial_step(field, east_speed, north_speed):
    channels, row_count, width = field.shape
    anywhere = pl.BlockSpec(memory_space=pl.ANY)
    payload = (channels, row_count + EXTRA, width)
    cols, rows = (2, channels // GROUP, GROUP * row_count), (2, channels, width)
    return pl.pallas_call(
        partial_kernel,
        out_shape=(
            jax.ShapeDtypeStruct(payload, jnp.bfloat16),
            jax.ShapeDtypeStruct(cols, jnp.float32),
            jax.ShapeDtypeStruct(rows, jnp.float32),
        ),
        in_specs=[anywhere] * 3,
        out_specs=(anywhere, anywhere, anywhere),
        scratch_shapes=[
            pltpu.VMEM(field.shape, jnp.float32),
            pltpu.VMEM((2, row_count, width), jnp.float32),
            pltpu.VMEM(payload, jnp.bfloat16),
            pltpu.VMEM(cols, jnp.float32),
            pltpu.VMEM(rows, jnp.float32),
            pltpu.SemaphoreType.DMA((channels // GROUP + 2,)),
            pltpu.SemaphoreType.DMA((channels // GROUP + 2,)),
        ],
        cost_estimate=pl.CostEstimate(flops=field.size * 9, bytes_accessed=field.size * 6, transcendentals=0),
    )(field, east_speed, north_speed)


def merge_kernel(back_ref, full_ref, out_ref, energy_ref, wide_ref, sems):
    del full_ref
    channels, row_count, width = out_ref.shape
    bottom = at_bottom()
    polar = jnp.logical_or(bottom, lax.axis_index("lat") == 0)
    shift = lax.rem(width - CAP * lax.axis_index("lon"), width)
    group = 8

    @pl.when(polar)
    def _():
        copies = []
        for g in range(channels // group):
            for c in range(g * group, (g + 1) * group):
                for t in range(row_count // 16):
                    at = jnp.where(bottom, row_count - 16 - 16 * t, 16 * t)
                    wide_ref[c, 16 * t : 16 * t + 16, :] = back_ref[
                        c, pl.ds(pl.multiple_of(at, 16), 16), :
                    ].astype(jnp.float32)
            here = pl.ds(g * group, group)
            copies.append(pltpu.make_async_copy(wide_ref.at[here], out_ref.at[here], sems.at[g]))
            copies[-1].start()
        total = jnp.zeros((EXTRA, width), jnp.float32)
        for c in range(channels):
            total = total + back_ref[c, row_count : row_count + EXTRA, :].astype(jnp.float32)
        energy = jnp.sum(total, axis=0, keepdims=True) * (1.0 / (channels * channels * width))
        energy = pltpu.roll(jnp.broadcast_to(energy, (8, width)), shift, 1)
        energy_ref[...] = energy[:1, :CAP]
        for copy in copies:
            copy.wait()

    @pl.when(jnp.logical_not(polar))
    def _():
        energy_ref[...] = jnp.zeros((1, CAP), jnp.float32)


def merge(back, full):
    channels, row_count, width = full.shape
    anywhere = pl.BlockSpec(memory_space=pl.ANY)
    return pl.pallas_call(
        merge_kernel,
        out_shape=(
            jax.ShapeDtypeStruct(full.shape, jnp.float32),
            jax.ShapeDtypeStruct((1, CAP), jnp.float32),
        ),
        in_specs=[VMEM, anywhere],
        out_specs=(anywhere, VMEM),
        input_output_aliases={1: 0},
        scratch_shapes=[pltpu.VMEM(full.shape, jnp.float32), pltpu.SemaphoreType.DMA((channels // 8,))],
        compiler_params=pltpu.CompilerParams(vmem_limit_bytes=16 * 1024 * 1024),
    )(back, full)


def step_kernel(
    field_any, east_any, north_any, up_ref, down_ref, west_col_ref, east_col_ref, out_any,
    field_ref, flat_ref, out_ref, col_ref, in_sems, out_sems,
):
    channels, row_count, width = field_ref.shape
    flat_copies, copies = brought(field_any, (east_any, north_any), field_ref, flat_ref, in_sems)
    lane = lax.broadcasted_iota(jnp.int32, (row_count, width), 1)
    row = lax.broadcasted_iota(jnp.int32, (row_count, width), 0)
    for c in range(channels):
        g, at = c // GROUP, row_count * (c % GROUP)
        col_ref[2 * c : 2 * c + 1, :row_count] = east_col_ref[g : g + 1, at : at + row_count]
        col_ref[2 * c + 1 : 2 * c + 2, :row_count] = west_col_ref[g : g + 1, at : at + row_count]
    cols = col_ref[...].T[:row_count, :]
    cols = jnp.concatenate([cols, jnp.zeros((row_count, width - 2 * channels), jnp.float32)], axis=1)
    for copy in flat_copies:
        copy.wait()
    east, north = 0.5 * flat_ref[0], 0.5 * flat_ref[1]
    to_east, to_west = DIFFUSION - east, DIFFUSION + east
    to_south, to_north = DIFFUSION - north, DIFFUSION + north
    sent = []
    for g, copy in enumerate(copies):
        copy.wait()
        for c in range(g * GROUP, (g + 1) * GROUP):
            cells = field_ref[c]
            rim = pltpu.roll(cols, (width - 2 * c - 1) % width, 1)
            west = jnp.where(lane == 0, rim, pltpu.roll(cells, 1, 1))
            east = jnp.where(lane == width - 1, rim, pltpu.roll(cells, width - 1, 1))
            up = jnp.where(row == 0, up_ref[c : c + 1, :], pltpu.roll(cells, 1, 0))
            down = jnp.where(row == row_count - 1, down_ref[c : c + 1, :], pltpu.roll(cells, row_count - 1, 0))
            out_ref[c] = (
                (1.0 - 4.0 * DIFFUSION) * cells + to_east * east + to_west * west + to_south * down + to_north * up
            )
        here = pl.ds(g * GROUP, GROUP)
        sent.append(pltpu.make_async_copy(out_ref.at[here], out_any.at[here], out_sems.at[g]))
        sent[-1].start()
    for copy in sent:
        copy.wait()


def step(field, east_speed, north_speed, up, down, west_col, east_col):
    channels, row_count, width = field.shape
    anywhere = pl.BlockSpec(memory_space=pl.ANY)
    return pl.pallas_call(
        step_kernel,
        out_shape=jax.ShapeDtypeStruct(field.shape, jnp.float32),
        in_specs=[anywhere] * 3 + [VMEM] * 4,
        out_specs=anywhere,
        scratch_shapes=[
            pltpu.VMEM(field.shape, jnp.float32),
            pltpu.VMEM((2, row_count, width), jnp.float32),
            pltpu.VMEM(field.shape, jnp.float32),
            pltpu.VMEM((2 * channels, width), jnp.float32),
            pltpu.SemaphoreType.DMA((channels // GROUP + 2,)),
            pltpu.SemaphoreType.DMA((channels // GROUP,)),
        ],
        cost_estimate=pl.CostEstimate(flops=field.size * 9, bytes_accessed=field.size * 8, transcendentals=0),
    )(field, east_speed, north_speed, up, down, west_col, east_col)


def on_device(lat_count, lon_count, atmosphere, east_speed, north_speed, owners, cutoff):
    channels, row_count, width = atmosphere.shape
    bottom = at_bottom()

    groups = [rank_order(lon_count)]
    exchange = functools.partial(
        lax.all_to_all, axis_name="lon", split_axis=0, concat_axis=0, tiled=True, axis_index_groups=groups
    )
    sent, cols, edge_rows = partial_step(atmosphere, east_speed, north_speed)
    received = exchange(sent)
    owner_row = jnp.where(bottom, owners[1, :, 0], owners[0, :, 0])
    cut_row = jnp.where(bottom, cutoff[1], cutoff[0])
    same = owner_row[:, None] == owner_row[None, :]
    earlier = lax.iota(jnp.int32, row_count)[:, None] > lax.iota(jnp.int32, row_count)[None, :]
    rank = jnp.sum(jnp.logical_and(same, earlier).astype(jnp.int32), axis=1)
    slot = owner_row * CAP + rank

    def placed(values):
        blocks = values.reshape(row_count // 16, 16)
        return jnp.where(bottom, blocks[::-1], blocks).reshape(row_count, 1)

    def next_band(rows):
        pairs = [(b * lon_count + o, (b ^ 1) * lon_count + o) for b in range(lat_count) for o in range(lon_count)]
        return lax.ppermute(rows[:, row_count + 5], ("lat", "lon"), pairs)

    west_col = lax.ppermute(cols[1], "lon", [(o, (o + 1) % lon_count) for o in range(lon_count)])
    east_col = lax.ppermute(cols[0], "lon", [((o + 1) % lon_count, o) for o in range(lon_count)])
    up = lax.ppermute(edge_rows[1], "lat", [(b, b + 1) for b in range(lat_count - 1)])
    down = lax.ppermute(edge_rows[0], "lat", [(b + 1, b) for b in range(lat_count - 1)])
    received, halos = lax.optimization_barrier((received, (up, down, west_col, east_col)))
    filtered = filter_rows(received, next_band, placed(cut_row), placed(slot))
    returned = exchange(filtered)
    full = step(atmosphere, east_speed, north_speed, *halos)
    return merge(returned, full)


def solution(mesh):
    in_specs = (P(None, "lat", "lon"), P("lat", "lon"), P("lat", "lon"), P(), P())
    out_specs = (P(None, "lat", "lon"), P("lat", "lon"))
    return jax.shard_map(
        functools.partial(on_device, mesh.shape["lat"], mesh.shape["lon"]),
        mesh=mesh,
        in_specs=in_specs,
        out_specs=out_specs,
        check_vma=False,
    )
```
